1024 devices in a mesh: member: 64 (over x, y_lo, core), lat: 16 (over z, y_hi).
Axes of the slice: x: 8, y: 8 (y_hi: 2, y_lo: 4; y = y_hi * 4 + y_lo), z: 8, core: 2. Of those that a mesh axis runs over, the one named last changes fastest.
Arguments:
- state: float32 [256, 128, 8, 256], P('member', 'lat'), may hold values from -6 to 6
- zonal_wind: float32 [128, 8, 256], P('lat'), may hold values from -5 to 5
- meridional_wind: float32 [128, 8, 256], P('lat'), may hold values from -5 to 5
- obs_cell: int32 [128, 8, 128], P('lat'), may hold values from 0 to 255
- obs_value: float32 [128, 8, 128], P('lat'), may hold values from -10 to 10
- obs_weight: float32 [128, 8, 128], P('lat'), may hold values from 1 to 1024
Outputs:
- analysis: float32 [256, 128, 8, 256], P('member', 'lat')
The draws below stay inside these ranges and needn't reach their ends.
All inputs are finite; a program needn't handle non-finite values.
Results may differ from the reference program's by a relative error of at most 0.00014.
Values sent between devices are 32-bit elements; how exact they have to be, the bound alone decides.
A program may use at most 32 MiB of HBM per device.

```python
import math
import jax
import jax.numpy as jnp
from jax import lax

MEMBERS = 256
NLAT = 128
LEV = 8
NLON = 256
OBS = 128
SWEEPS = 3


def set_ends(array, stream_key, least, high):
    extent = array.shape
    index_at = [jax.random.randint(jax.random.fold_in(stream_key, axis), (), 0, extent[axis]) for axis in range(len(extent))]
    array = array.at[tuple(index_at)].set(least)
    longest = extent.index(max(extent))
    index_at[longest] = (index_at[longest] + 1) % extent[longest]
    return array.at[tuple(index_at)].set(high)


def levels(key, shape, split, least, high):
    loudness = 1.0
    for position, blocks in split:
        draws = jax.random.uniform(jax.random.fold_in(jax.random.fold_in(key, 6), position), (blocks,), jnp.float32, least / len(split), high / len(split))
        loudness = loudness * jnp.repeat(jnp.exp(draws), shape[position] // blocks).reshape((-1,) + (1,) * (len(shape) - 1 - position))
    return loudness


def gaussian(rng, dims, spread, limit, cuts=(), held_as=jnp.bfloat16):
    gain = levels(rng, dims, cuts, -0.22, 0.18) if cuts else 1.0
    array = jax.random.normal(rng, dims, jnp.float32) * spread * gain
    return jnp.minimum(jnp.maximum(array, -limit), limit).astype(held_as)


def setup_inputs(seed: int = 0) -> dict:
    splits = jax.random.split(jax.random.key(seed), 7)
    return {
        "state": gaussian(splits[0], (MEMBERS, NLAT, LEV, NLON), 1.0, 6.0, ((0, 64), (1, 16)), jnp.float32),
        "zonal_wind": gaussian(splits[1], (NLAT, LEV, NLON), 1.0, 5.0, ((0, 16),), jnp.float32),
        "meridional_wind": gaussian(splits[2], (NLAT, LEV, NLON), 1.0, 5.0, ((0, 16),), jnp.float32),
        "obs_cell": set_ends(jax.random.randint(splits[3], (NLAT, LEV, OBS), 0, NLON), jax.random.fold_in(splits[3], 1), 0, NLON - 1).astype(jnp.int32),
        "obs_value": gaussian(splits[4], (NLAT, LEV, OBS), 2.0, 10.0, ((0, 16),), jnp.float32),
        "obs_weight": jnp.clip(jnp.exp(math.log(1024.0) - 6.931472 * jax.random.uniform(splits[5], (NLAT, LEV, OBS), jnp.float32) ** levels(splits[5], (NLAT, LEV, OBS), ((0, 16),), -0.2, 0.2)), 1.0, 1024.0),
    }


step_size = 0.3

def advance(padded, zonal, meridional):
    middle = padded[:, 1:-1]
    north_row = padded[:, 2:]
    south_row = padded[:, :-2]
    east_cell = jnp.roll(middle, -1, axis=3)
    west_cell = jnp.roll(middle, 1, axis=3)
    return middle - step_size * ((zonal + middle) * (east_cell - west_cell) * 0.5 + meridional * (north_row - south_row) * 0.5)

def analyse(ensemble, observed, values, weights):
    highest = lax.Precision.HIGHEST
    count = ensemble.shape[0]
    obs_mean = lax.optimization_barrier(jnp.mean(observed, axis=0))
    perturb = observed - obs_mean
    innovation = values - obs_mean
    gram = jnp.einsum('kro,lro->rkl', perturb * weights, perturb, precision=highest)
    identity = jnp.eye(count, dtype=jnp.float32)
    system = gram + (count - 1.0) * identity
    frobenius = jnp.sqrt(lax.optimization_barrier(jnp.sum(system * system, axis=(1, 2))))
    iterate = system / frobenius[:, None, None]
    inverse = jnp.broadcast_to(identity, system.shape)
    for sweep in range(SWEEPS):
        product = jnp.einsum('rij,rjk->rik', inverse, iterate, precision=highest)
        factor = 1.5 * identity - 0.5 * product
        iterate = jnp.einsum('rij,rjk->rik', iterate, factor, precision=highest)
        inverse = jnp.einsum('rij,rjk->rik', factor, inverse, precision=highest)
    root = inverse / jnp.sqrt(frobenius)[:, None, None]
    covariance = jnp.einsum('rij,rjk->rik', root, root, precision=highest)
    projected = jnp.einsum('kro,ro->rk', perturb, weights * innovation, precision=highest)
    mean_weights = jnp.einsum('rkl,rl->rk', covariance, projected, precision=highest)
    transform = mean_weights[:, :, None] + jnp.sqrt(count - 1.0) * root
    state_mean = lax.optimization_barrier(jnp.mean(ensemble, axis=0))
    state_pert = ensemble - state_mean
    return state_mean + jnp.einsum('rkm,krn->mrn', transform, state_pert, precision=highest)

def reference(state, zonal_wind, meridional_wind, obs_cell, obs_value, obs_weight):
    count = state.shape[0]
    field = state
    for iteration in range(2):
        padded = jnp.pad(field, ((0, 0), (1, 1), (0, 0), (0, 0)))
        field = advance(padded, zonal_wind, meridional_wind)
    latitude_rows = jnp.transpose(field, (1, 0, 2, 3))

    def one_row(items):
        band_rows, cells, values, weights = items
        picked = jnp.take_along_axis(band_rows, jnp.broadcast_to(cells[None], (count,) + cells.shape), axis=2)
        return analyse(band_rows, picked, values, weights)
    result = lax.map(one_row, (latitude_rows, obs_cell, obs_value, obs_weight))
    return jnp.transpose(result, (1, 0, 2, 3))
```

```python
import math

import jax
import jax.numpy as jnp
from jax import lax
from jax.experimental import pallas as pl
from jax.experimental.pallas import tpu as pltpu
from jax.sharding import PartitionSpec as P

MESH = pl.DeviceIdType.MESH
F32 = jnp.float32
BF16 = jnp.bfloat16
HALF_STEP = 0.15
LANES = 128


def split(x):
    high = x.astype(BF16)
    low = (x - high.astype(F32)).astype(BF16)
    return high, low


def dot(a, b):
    return lax.dot_general(a, b, (((1,), (0,)), ((), ())), preferred_element_type=F32)


def dot3(a, b):
    return dot(a[0], b[0]) + (dot(a[0], b[1]) + dot(a[1], b[0]))


def analyse(ensemble, cells, values, weights):
    count, lons = ensemble.shape
    obs = cells.shape[1]
    inflate = count - 1.0
    mean = jnp.sum(ensemble, axis=0, keepdims=True) * (1.0 / count)
    pert = ensemble - mean
    pick = jnp.where(lax.broadcasted_iota(jnp.int32, (lons, obs), 0) == cells, 1.0, 0.0).astype(BF16)
    pert_s = split(pert)
    picked = dot(pert_s[0], pick) + dot(pert_s[1], pick)
    mean_s = split(jnp.broadcast_to(mean, (8, lons)))
    obs_mean = dot(mean_s[0], pick) + dot(mean_s[1], pick)
    root_weight = jnp.sqrt(weights)
    scaled = picked * root_weight
    target = (values - obs_mean) * root_weight
    scaled_s = split(scaled)
    turned_s = (scaled_s[0].T, scaled_s[1].T)
    gram = dot3(turned_s, scaled_s)
    cross = dot3(turned_s, pert_s)
    trace = jnp.sum(jnp.sum(scaled * scaled, axis=0, keepdims=True), axis=1, keepdims=True)
    square = jnp.sum(jnp.sum(gram * gram, axis=0, keepdims=True), axis=1, keepdims=True)
    frob = jnp.sqrt(square + 2.0 * inflate * trace + inflate * inflate * count)
    unit = 1.0 / frob
    a0 = inflate * unit
    p1 = 1.5 - 0.5 * a0
    q2 = a0 * p1 * p1
    p2 = 1.5 - 0.5 * q2
    q3 = q2 * p2 * p2
    p3 = 1.5 - 0.5 * q3
    z0 = p1 * p2 * p3
    diagonal = lax.broadcasted_iota(jnp.int32, (obs, obs), 0) == lax.broadcasted_iota(jnp.int32, (obs, obs), 1)
    eye = jnp.where(diagonal, 1.0, 0.0)
    s = gram * unit
    s_s = split(s)
    s2 = dot3(s_s, s_s)
    t2 = (p1 * p1 - a0 * p1) * eye + (0.25 * a0 - p1) * s + 0.25 * s2
    m2 = dot3(s_s, split(t2))
    f2 = p2 * eye - 0.5 * m2
    e = p1 * t2 - 0.5 * m2
    f2_s = split(f2)
    u = dot3(f2_s, f2_s) - (0.5 * q2) * (f2 + p2 * eye)
    k = dot3(f2_s, split(e))
    r = -0.5 * (dot3(split(u), split(k)) + p3 * e + (p3 * p2) * eye)
    r_s = split(r)
    core_s = split(dot3(r_s, split(cross)))
    target_s = split(target)
    lead = 2.0 * z0 * dot3(target_s, s_s) + dot3(split(dot3(target_s, split(s2))), r_s)
    shift = unit * (z0 * z0 * dot3(target_s, split(cross)) + dot3(split(lead), core_s))
    gain = jnp.sqrt(inflate * unit)
    return (mean + shift[:1]) + (gain * z0) * pert + (gain * unit) * dot3(scaled_s, core_s)


def around(x, shift):
    lons = x.shape[-1]
    return pltpu.roll(x.reshape(-1, lons), shift, 1).reshape(x.shape)


def slope(x):
    return around(x, x.shape[-1] - 1) - around(x, 1)


def flow(x, zonal):
    return x - (HALF_STEP * (zonal + x)) * slope(x)


def kernel(groups, bands, state, zonal, merid, cell, value, weight, out,
           q, u, v, cells, values, weights, low_out, high_out, low_in, high_in,
           inner, outer, gathered, result, returned,
           load_sem, halo_send, halo_recv, go_send, go_recv, back_send, back_recv, own_sem):
    me = lax.axis_index("member")
    band = lax.axis_index("lat")
    members, rows, levels, lons = state.shape
    halves = lons // LANES
    index = me // 2
    odd = me % 2
    turn = index // levels
    my_row = jnp.where(odd == 0, rows // 4 + turn, turn + (turn // 2) * (rows // 2))
    my_level = index % levels

    loads = [
        pltpu.make_async_copy(state, q, load_sem.at[0]),
        pltpu.make_async_copy(zonal, u, load_sem.at[1]),
        pltpu.make_async_copy(merid, v, load_sem.at[2]),
        pltpu.make_async_copy(cell.at[my_row], cells, load_sem.at[3]),
        pltpu.make_async_copy(value.at[my_row], values, load_sem.at[4]),
        pltpu.make_async_copy(weight.at[my_row], weights, load_sem.at[5]),
    ]
    for load in loads:
        load.start()

    barrier = pltpu.get_barrier_semaphore()
    below, above = band > 0, band < bands - 1

    @pl.when(below)
    def _():
        pl.semaphore_signal(barrier, inc=1, device_id={"lat": band - 1}, device_id_type=MESH)

    @pl.when(above)
    def _():
        pl.semaphore_signal(barrier, inc=1, device_id={"lat": band + 1}, device_id_type=MESH)

    def greet(step, carry):
        pl.semaphore_signal(barrier, inc=1, device_id={"member": lax.rem(me + step, groups)}, device_id_type=MESH)
        return carry

    lax.fori_loop(1, groups, greet, 0)

    for load in loads[:3]:
        load.wait()

    wind_v = HALF_STEP * v[...]
    wind_u = u[...]

    first, last = q[:, 0], q[:, rows - 1]
    low_out[:members] = first
    low_out[members : 2 * members] = flow(first, wind_u[0]) - wind_v[0] * q[:, 1]
    low_out[2 * members] = wind_v[0]
    high_out[:members] = last
    high_out[members : 2 * members] = flow(last, wind_u[rows - 1]) + wind_v[rows - 1] * q[:, rows - 2]
    high_out[2 * members] = wind_v[rows - 1]

    pl.semaphore_wait(barrier, groups - 1 + below.astype(jnp.int32) + above.astype(jnp.int32))

    def to_low():
        return pltpu.make_async_remote_copy(
            src_ref=low_out, dst_ref=high_in, send_sem=halo_send.at[0], recv_sem=halo_recv.at[0],
            device_id={"lat": band - 1}, device_id_type=MESH)

    def to_high():
        return pltpu.make_async_remote_copy(
            src_ref=high_out, dst_ref=low_in, send_sem=halo_send.at[1], recv_sem=halo_recv.at[1],
            device_id={"lat": band + 1}, device_id_type=MESH)

    @pl.when(below)
    def _():
        to_low().start()

    @pl.when(above)
    def _():
        to_high().start()

    def advance(x, top, bottom, row, length):
        return flow(x, wind_u[row : row + length]) - wind_v[row : row + length] * (top - bottom)

    def put(block, x, place):
        for half in range(halves):
            for member in range(members):
                block[pl.ds(place * 8 + half * members + member, levels, stride=8), :] = (
                    x[member, :, half * LANES : (half + 1) * LANES])

    old = q[...]
    mid = advance(old[:, 1 : rows - 1], old[:, 2:], old[:, : rows - 2], 1, rows - 2)
    new = advance(mid[:, 1 : rows - 3], mid[:, 2:], mid[:, : rows - 4], 2, rows - 4)
    for row in range(rows - 4):
        put(inner, new[:, row], row * levels)

    def send(block, parity):
        def go(step, carry):
            place = lax.rem(index + step, groups // 2)
            peer = 2 * place + parity

            @pl.when(peer != me)
            def _():
                pltpu.make_async_remote_copy(
                    src_ref=block.at[pl.ds(pl.multiple_of(place * 8, 8), 8)],
                    dst_ref=gathered.at[pl.ds(pl.multiple_of(me * 8, 8), 8)],
                    send_sem=go_send, recv_sem=go_recv, device_id={"member": peer}, device_id_type=MESH).start()

            return carry

        lax.fori_loop(0, groups // 2, go, 0)

    def keep(block):
        return pltpu.make_async_copy(
            block.at[pl.ds(pl.multiple_of(index * 8, 8), 8)],
            gathered.at[pl.ds(pl.multiple_of(me * 8, 8), 8)], own_sem.at[0])

    send(inner, 0)

    @pl.when(below)
    def _():
        to_high().wait_recv()

    @pl.when(band == 0)
    def _():
        low_in[...] = jnp.zeros_like(low_in)

    @pl.when(above)
    def _():
        to_low().wait_recv()

    @pl.when(band == bands - 1)
    def _():
        high_in[...] = jnp.zeros_like(high_in)

    before = low_in[members : 2 * members] - low_in[2 * members] * first
    after = high_in[members : 2 * members] + high_in[2 * members] * last
    row0 = flow(first, wind_u[0]) - wind_v[0] * (old[:, 1] - low_in[:members])
    row7 = flow(last, wind_u[rows - 1]) - wind_v[rows - 1] * (high_in[:members] - old[:, rows - 2])
    put(outer, flow(row0, wind_u[0]) - wind_v[0] * (mid[:, 0] - before), 0)
    put(outer, flow(mid[:, 0], wind_u[1]) - wind_v[1] * (mid[:, 1] - row0), levels)
    put(outer, flow(mid[:, rows - 3], wind_u[rows - 2]) - wind_v[rows - 2] * (row7 - mid[:, rows - 4]), 2 * levels)
    put(outer, flow(row7, wind_u[rows - 1]) - wind_v[rows - 1] * (after - mid[:, rows - 3]), 3 * levels)
    send(outer, 1)

    @pl.when(odd == 0)
    def _():
        keep(inner).start()

    @pl.when(odd == 1)
    def _():
        keep(outer).start()

    keep(inner).wait()
    for load in loads[3:]:
        load.wait()
    others = (groups - 1) * 8
    pltpu.make_async_copy(gathered.at[pl.ds(0, others)], gathered.at[pl.ds(0, others)], go_recv).wait()

    ensemble = jnp.concatenate(
        [jnp.concatenate(
            [gathered[pl.ds(half * members + member, groups, stride=8), :] for member in range(members)], axis=0)
         for half in range(halves)], axis=1)
    analysed = analyse(
        ensemble, cells[pl.ds(my_level, 1), :], values[pl.ds(my_level, 1), :], weights[pl.ds(my_level, 1), :])
    for half in range(halves):
        for member in range(members):
            result[pl.ds(half * members + member, groups, stride=8), :] = (
                analysed[member * groups : (member + 1) * groups, half * LANES : (half + 1) * LANES])

    mine = pl.ds(pl.multiple_of(me * 8, 8), 8)

    def give(step, carry):
        peer = lax.rem(me + step, groups)
        pltpu.make_async_remote_copy(
            src_ref=result.at[pl.ds(pl.multiple_of(peer * 8, 8), 8)], dst_ref=returned.at[mine],
            send_sem=back_send, recv_sem=back_recv, device_id={"member": peer}, device_id_type=MESH).start()
        return carry

    lax.fori_loop(1, groups, give, 0)
    own = pltpu.make_async_copy(result.at[mine], returned.at[mine], own_sem.at[1])
    own.start()
    own.wait()
    pltpu.make_async_copy(returned.at[pl.ds(0, others)], returned.at[pl.ds(0, others)], back_recv).wait()

    for row in range(rows):
        parity = 0 if rows // 4 <= row < rows - rows // 4 else 1
        block = row - rows // 4 if parity == 0 else (row if row < rows // 4 else row - rows // 2)
        for half in range(halves):
            for member in range(members):
                start = (2 * block * levels + parity) * 8 + half * members + member
                out[member, row, :, half * LANES : (half + 1) * LANES] = returned[pl.ds(start, levels, stride=16), :]

    @pl.when(below)
    def _():
        to_low().wait_send()

    @pl.when(above)
    def _():
        to_high().wait_send()

    pltpu.make_async_copy(gathered.at[pl.ds(0, others)], gathered.at[pl.ds(0, others)], go_send).wait()
    pltpu.make_async_copy(returned.at[pl.ds(0, others)], returned.at[pl.ds(0, others)], back_send).wait()


def solution(mesh):
    groups, bands = mesh.shape["member"], mesh.shape["lat"]

    def body(state, zonal, merid, cell, value, weight):
        members, rows, levels, lons = state.shape
        obs = cell.shape[-1]
        halo = (2 * members + 1, levels, lons)
        tiles = groups * 8
        return pl.pallas_call(
            lambda *refs: kernel(groups, bands, *refs),
            out_shape=jax.ShapeDtypeStruct(state.shape, F32),
            in_specs=[pl.BlockSpec(memory_space=pl.ANY)] * 6,
            out_specs=pl.BlockSpec(memory_space=pltpu.VMEM),
            scratch_shapes=[
                pltpu.VMEM(state.shape, F32),
                pltpu.VMEM(zonal.shape, F32),
                pltpu.VMEM(merid.shape, F32),
                pltpu.VMEM((levels, obs), jnp.int32),
                pltpu.VMEM((levels, obs), F32),
                pltpu.VMEM((levels, obs), F32),
                pltpu.VMEM(halo, F32),
                pltpu.VMEM(halo, F32),
                pltpu.VMEM(halo, F32),
                pltpu.VMEM(halo, F32),
                pltpu.VMEM((tiles // 2, LANES), F32),
                pltpu.VMEM((tiles // 2, LANES), F32),
                pltpu.VMEM((tiles, LANES), F32),
                pltpu.VMEM((tiles, LANES), F32),
                pltpu.VMEM((tiles, LANES), F32),
                pltpu.SemaphoreType.DMA((6,)),
                pltpu.SemaphoreType.DMA((2,)),
                pltpu.SemaphoreType.DMA((2,)),
                pltpu.SemaphoreType.DMA,
                pltpu.SemaphoreType.DMA,
                pltpu.SemaphoreType.DMA,
                pltpu.SemaphoreType.DMA,
                pltpu.SemaphoreType.DMA((2,)),
            ],
            compiler_params=pltpu.CompilerParams(collective_id=0, has_side_effects=True, vmem_limit_bytes=32 * 1024 * 1024),
        )(state, zonal, merid, cell, value, weight)

    in_specs = (P("member", "lat", None, None),) + (P("lat", None, None),) * 5
    return jax.shard_map(body, mesh=mesh, in_specs=in_specs, out_specs=P("member", "lat", None, None), check_vma=False)
```

```python
import math

import jax
import jax.numpy as jnp
from jax import lax
from jax.experimental import pallas as pl
from jax.experimental.pallas import tpu as pltpu
from jax.sharding import PartitionSpec as P

MESH = pl.DeviceIdType.MESH
F32 = jnp.float32
BF16 = jnp.bfloat16
HALF_STEP = 0.15
LANES = 128


def split(x):
    high = x.astype(BF16)
    low = (x - high.astype(F32)).astype(BF16)
    return high, low


def dot(a, b):
    return lax.dot_general(a, b, (((1,), (0,)), ((), ())), preferred_element_type=F32)


def dot3(a, b):
    return dot(a[0], b[0]) + (dot(a[0], b[1]) + dot(a[1], b[0]))


def analyse(ensemble, cells, values, weights):
    count, lons = ensemble.shape
    obs = cells.shape[1]
    inflate = count - 1.0
    mean = jnp.sum(ensemble, axis=0, keepdims=True) * (1.0 / count)
    pert = ensemble - mean
    pick = jnp.where(lax.broadcasted_iota(jnp.int32, (lons, obs), 0) == cells, 1.0, 0.0).astype(BF16)
    pert_s = split(pert)
    picked = dot(pert_s[0], pick) + dot(pert_s[1], pick)
    mean_s = split(jnp.broadcast_to(mean, (8, lons)))
    obs_mean = dot(mean_s[0], pick) + dot(mean_s[1], pick)
    root_weight = jnp.sqrt(weights)
    scaled = picked * root_weight
    target = (values - obs_mean) * root_weight
    scaled_s = split(scaled)
    turned_s = (scaled_s[0].T, scaled_s[1].T)
    gram = dot3(turned_s, scaled_s)
    cross = dot3(turned_s, pert_s)
    trace = jnp.sum(jnp.sum(scaled * scaled, axis=0, keepdims=True), axis=1, keepdims=True)
    square = jnp.sum(jnp.sum(gram * gram, axis=0, keepdims=True), axis=1, keepdims=True)
    frob = jnp.sqrt(square + 2.0 * inflate * trace + inflate * inflate * count)
    unit = 1.0 / frob
    a0 = inflate * unit
    p1 = 1.5 - 0.5 * a0
    q2 = a0 * p1 * p1
    p2 = 1.5 - 0.5 * q2
    q3 = q2 * p2 * p2
    p3 = 1.5 - 0.5 * q3
    z0 = p1 * p2 * p3
    diagonal = lax.broadcasted_iota(jnp.int32, (obs, obs), 0) == lax.broadcasted_iota(jnp.int32, (obs, obs), 1)
    eye = jnp.where(diagonal, 1.0, 0.0)
    s = gram * unit
    s_s = split(s)
    s2 = dot3(s_s, s_s)
    t2 = (p1 * p1 - a0 * p1) * eye + (0.25 * a0 - p1) * s + 0.25 * s2
    m2 = dot3(s_s, split(t2))
    f2 = p2 * eye - 0.5 * m2
    e = p1 * t2 - 0.5 * m2
    f2_s = split(f2)
    u = dot3(f2_s, f2_s) - (0.5 * q2) * (f2 + p2 * eye)
    k = dot3(f2_s, split(e))
    r = -0.5 * (dot3(split(u), split(k)) + p3 * e + (p3 * p2) * eye)
    r_s = split(r)
    core_s = split(dot3(r_s, split(cross)))
    target_s = split(target)
    lead = 2.0 * z0 * dot3(target_s, s_s) + dot3(split(dot3(target_s, split(s2))), r_s)
    shift = unit * (z0 * z0 * dot3(target_s, split(cross)) + dot3(split(lead), core_s))
    gain = jnp.sqrt(inflate * unit)
    return (mean + shift[:1]) + (gain * z0) * pert + (gain * unit) * dot3(scaled_s, core_s)


def around(x, shift):
    lons = x.shape[-1]
    return pltpu.roll(x.reshape(-1, lons), shift, 1).reshape(x.shape)


def slope(x):
    return around(x, x.shape[-1] - 1) - around(x, 1)


def flow(x, zonal):
    return x - (HALF_STEP * (zonal + x)) * slope(x)


def kernel(groups, bands, state, zonal, merid, cell, value, weight, out,
           q, u, v, cells, values, weights, low_out, high_out, low_in, high_in,
           inner, outer, gathered, result, returned,
           load_sem, halo_send, halo_recv, go_send, go_recv, back_send, back_recv, own_sem, ready, band_ready):
    me = lax.axis_index("member")
    band = lax.axis_index("lat")
    members, rows, levels, lons = state.shape
    halves = lons // LANES
    index = me // 2
    odd = me % 2
    turn = index // levels
    my_row = jnp.where(odd == 0, rows // 4 + turn, turn + (turn // 2) * (rows // 2))
    my_level = index % levels

    loads = [
        pltpu.make_async_copy(state, q, load_sem.at[0]),
        pltpu.make_async_copy(zonal, u, load_sem.at[1]),
        pltpu.make_async_copy(merid, v, load_sem.at[2]),
        pltpu.make_async_copy(cell.at[my_row], cells, load_sem.at[3]),
        pltpu.make_async_copy(value.at[my_row], values, load_sem.at[4]),
        pltpu.make_async_copy(weight.at[my_row], weights, load_sem.at[5]),
    ]
    for load in loads:
        load.start()

    barrier = pltpu.get_barrier_semaphore()
    below, above = band > 0, band < bands - 1
    peers_x, peers_y = groups // 8, 4
    my_x, my_y = index // peers_y, index % peers_y

    @pl.when(below)
    def _():
        pl.semaphore_signal(barrier, inc=1, device_id={"lat": band - 1}, device_id_type=MESH)

    def greet(step, carry):
        peer = lax.rem(me + step, groups)

        @pl.when(me > 0)
        def _():
            pl.semaphore_signal(barrier, inc=1, device_id={"member": peer}, device_id_type=MESH)

        return carry

    lax.fori_loop(1, groups, greet, 0)

    for load in loads[:3]:
        load.wait()

    wind_v = HALF_STEP * v[...]
    wind_u = u[...]

    first, last = q[:, 0], q[:, rows - 1]
    low_out[:members] = first
    low_out[members : 2 * members] = flow(first, wind_u[0]) - wind_v[0] * q[:, 1]
    low_out[2 * members] = wind_v[0]
    high_out[:members] = last
    high_out[members : 2 * members] = flow(last, wind_u[rows - 1]) + wind_v[rows - 1] * q[:, rows - 2]
    high_out[2 * members] = wind_v[rows - 1]

    pl.semaphore_wait(barrier, groups - 2 + (me == 0).astype(jnp.int32) + above.astype(jnp.int32))

    @pl.when(above)
    def _():
        pl.semaphore_signal(band_ready, inc=1, device_id={"lat": band + 1}, device_id_type=MESH)

    @pl.when(me == 0)
    def _():
        def answer(step, carry):
            pl.semaphore_signal(ready, inc=1, device_id={"member": step}, device_id_type=MESH)
            return carry

        lax.fori_loop(1, groups, answer, 0)


    def to_low():
        return pltpu.make_async_remote_copy(
            src_ref=low_out, dst_ref=high_in, send_sem=halo_send.at[0], recv_sem=halo_recv.at[0],
            device_id={"lat": band - 1}, device_id_type=MESH)

    def to_high():
        return pltpu.make_async_remote_copy(
            src_ref=high_out, dst_ref=low_in, send_sem=halo_send.at[1], recv_sem=halo_recv.at[1],
            device_id={"lat": band + 1}, device_id_type=MESH)

    @pl.when(above)
    def _():
        to_high().start()

    def advance(x, top, bottom, row, length):
        return flow(x, wind_u[row : row + length]) - wind_v[row : row + length] * (top - bottom)

    def put(block, x, place):
        for half in range(halves):
            for member in range(members):
                block[pl.ds(place * 8 + half * members + member, levels, stride=8), :] = (
                    x[member, :, half * LANES : (half + 1) * LANES])

    old = q[...]
    mid = advance(old[:, 1 : rows - 1], old[:, 2:], old[:, : rows - 2], 1, rows - 2)
    new = advance(mid[:, 1 : rows - 3], mid[:, 2:], mid[:, : rows - 4], 2, rows - 4)
    for row in range(rows - 4):
        put(inner, new[:, row], row * levels)

    def place_of(step):
        turn = step // peers_y
        far = peers_x // 2 + ((turn + 1) // 2) * (2 * (turn % 2) - 1)
        return lax.rem(my_x + far, peers_x) * peers_y + lax.rem(my_y + 1 + step, peers_y)

    def go(block, place, parity):
        return pltpu.make_async_remote_copy(
            src_ref=block.at[pl.ds(pl.multiple_of(place * 8, 8), 8)],
            dst_ref=gathered.at[pl.ds(pl.multiple_of(me * 8, 8), 8)],
            send_sem=go_send, recv_sem=go_recv, device_id={"member": 2 * place + parity}, device_id_type=MESH)

    def send(block, parity):
        def start(step, carry):
            place = place_of(step)
            peer = 2 * place + parity

            @pl.when((peer != me) & (peer > 0))
            def _():
                go(block, place, parity).start()

            return carry

        lax.fori_loop(0, groups // 2, start, 0)

    def keep(block):
        return pltpu.make_async_copy(
            block.at[pl.ds(pl.multiple_of(index * 8, 8), 8)],
            gathered.at[pl.ds(pl.multiple_of(me * 8, 8), 8)], own_sem.at[0])

    send(inner, 0)

    @pl.when(below)
    def _():
        pl.semaphore_wait(band_ready, 1)
        to_low().start()

    @pl.when(below)
    def _():
        to_high().wait_recv()

    @pl.when(band == 0)
    def _():
        low_in[...] = jnp.zeros_like(low_in)

    @pl.when(above)
    def _():
        to_low().wait_recv()

    @pl.when(band == bands - 1)
    def _():
        high_in[...] = jnp.zeros_like(high_in)

    before = low_in[members : 2 * members] - low_in[2 * members] * first
    after = high_in[members : 2 * members] + high_in[2 * members] * last
    row0 = flow(first, wind_u[0]) - wind_v[0] * (old[:, 1] - low_in[:members])
    row7 = flow(last, wind_u[rows - 1]) - wind_v[rows - 1] * (high_in[:members] - old[:, rows - 2])
    put(outer, flow(row0, wind_u[0]) - wind_v[0] * (mid[:, 0] - before), 0)
    put(outer, flow(mid[:, 0], wind_u[1]) - wind_v[1] * (mid[:, 1] - row0), levels)
    put(outer, flow(mid[:, rows - 3], wind_u[rows - 2]) - wind_v[rows - 2] * (row7 - mid[:, rows - 4]), 2 * levels)
    put(outer, flow(row7, wind_u[rows - 1]) - wind_v[rows - 1] * (after - mid[:, rows - 3]), 3 * levels)
    send(outer, 1)

    @pl.when(me > 0)
    def _():
        pl.semaphore_wait(ready, 1)
        go(inner, 0, 0).start()

    @pl.when(odd == 0)
    def _():
        keep(inner).start()

    @pl.when(odd == 1)
    def _():
        keep(outer).start()

    keep(inner).wait()
    for load in loads[3:]:
        load.wait()
    others = (groups - 1) * 8
    pltpu.make_async_copy(gathered.at[pl.ds(0, others)], gathered.at[pl.ds(0, others)], go_recv).wait()

    ensemble = jnp.concatenate(
        [jnp.concatenate(
            [gathered[pl.ds(half * members + member, groups, stride=8), :] for member in range(members)], axis=0)
         for half in range(halves)], axis=1)
    analysed = analyse(
        ensemble, cells[pl.ds(my_level, 1), :], values[pl.ds(my_level, 1), :], weights[pl.ds(my_level, 1), :])
    for half in range(halves):
        for member in range(members):
            result[pl.ds(half * members + member, groups, stride=8), :] = (
                analysed[member * groups : (member + 1) * groups, half * LANES : (half + 1) * LANES])

    mine = pl.ds(pl.multiple_of(me * 8, 8), 8)

    def give(step, carry):
        peer = 2 * place_of(step // 2) + lax.rem(me + 1 + step, 2)

        @pl.when(peer != me)
        def _():
            pltpu.make_async_remote_copy(
                src_ref=result.at[pl.ds(pl.multiple_of(peer * 8, 8), 8)], dst_ref=returned.at[mine],
                send_sem=back_send, recv_sem=back_recv, device_id={"member": peer}, device_id_type=MESH).start()

        return carry

    lax.fori_loop(0, groups, give, 0)
    own = pltpu.make_async_copy(result.at[mine], returned.at[mine], own_sem.at[1])
    own.start()
    own.wait()
    pltpu.make_async_copy(returned.at[pl.ds(0, others)], returned.at[pl.ds(0, others)], back_recv).wait()

    for row in range(rows):
        parity = 0 if rows // 4 <= row < rows - rows // 4 else 1
        block = row - rows // 4 if parity == 0 else (row if row < rows // 4 else row - rows // 2)
        for half in range(halves):
            for member in range(members):
                start = (2 * block * levels + parity) * 8 + half * members + member
                out[member, row, :, half * LANES : (half + 1) * LANES] = returned[pl.ds(start, levels, stride=16), :]

    @pl.when(below)
    def _():
        to_low().wait_send()

    @pl.when(above)
    def _():
        to_high().wait_send()

    pltpu.make_async_copy(gathered.at[pl.ds(0, others)], gathered.at[pl.ds(0, others)], go_send).wait()
    pltpu.make_async_copy(returned.at[pl.ds(0, others)], returned.at[pl.ds(0, others)], back_send).wait()


def solution(mesh):
    groups, bands = mesh.shape["member"], mesh.shape["lat"]

    def body(state, zonal, merid, cell, value, weight):
        members, rows, levels, lons = state.shape
        obs = cell.shape[-1]
        halo = (2 * members + 1, levels, lons)
        tiles = groups * 8
        return pl.pallas_call(
            lambda *refs: kernel(groups, bands, *refs),
            out_shape=jax.ShapeDtypeStruct(state.shape, F32),
            in_specs=[pl.BlockSpec(memory_space=pl.ANY)] * 6,
            out_specs=pl.BlockSpec(memory_space=pltpu.VMEM),
            scratch_shapes=[
                pltpu.VMEM(state.shape, F32),
                pltpu.VMEM(zonal.shape, F32),
                pltpu.VMEM(merid.shape, F32),
                pltpu.VMEM((levels, obs), jnp.int32),
                pltpu.VMEM((levels, obs), F32),
                pltpu.VMEM((levels, obs), F32),
                pltpu.VMEM(halo, F32),
                pltpu.VMEM(halo, F32),
                pltpu.VMEM(halo, F32),
                pltpu.VMEM(halo, F32),
                pltpu.VMEM((tiles // 2, LANES), F32),
                pltpu.VMEM((tiles // 2, LANES), F32),
                pltpu.VMEM((tiles, LANES), F32),
                pltpu.VMEM((tiles, LANES), F32),
                pltpu.VMEM((tiles, LANES), F32),
                pltpu.SemaphoreType.DMA((6,)),
                pltpu.SemaphoreType.DMA((2,)),
                pltpu.SemaphoreType.DMA((2,)),
                pltpu.SemaphoreType.DMA,
                pltpu.SemaphoreType.DMA,
                pltpu.SemaphoreType.DMA,
                pltpu.SemaphoreType.DMA,
                pltpu.SemaphoreType.DMA((2,)),
                pltpu.SemaphoreType.REGULAR,
                pltpu.SemaphoreType.REGULAR,
            ],
            compiler_params=pltpu.CompilerParams(collective_id=0, has_side_effects=True, vmem_limit_bytes=60 * 1024 * 1024),
        )(state, zonal, merid, cell, value, weight)

    in_specs = (P("member", "lat", None, None),) + (P("lat", None, None),) * 5
    return jax.shard_map(body, mesh=mesh, in_specs=in_specs, out_specs=P("member", "lat", None, None), check_vma=False)
```

```python
import math

import jax
import jax.numpy as jnp
from jax import lax
from jax.experimental import pallas as pl
from jax.experimental.pallas import tpu as pltpu
from jax.sharding import PartitionSpec as P

MESH = pl.DeviceIdType.MESH
F32 = jnp.float32
BF16 = jnp.bfloat16
HALF_STEP = 0.15
LANES = 128
SIDE_X, SIDE_Y = 8, 4
FAR_X = (4, 5, 3, 6, 2, 7, 1, 0)
FAR_Y = (2, 1, 3, 0)


def split(x):
    high = x.astype(BF16)
    low = (x - high.astype(F32)).astype(BF16)
    return high, low


def dot(a, b):
    return lax.dot_general(a, b, (((1,), (0,)), ((), ())), preferred_element_type=F32)


def dot3(a, b):
    return dot(a[0], b[0]) + (dot(a[0], b[1]) + dot(a[1], b[0]))


def analyse(ensemble, cells, values, weights):
    count, lons = ensemble.shape
    obs = cells.shape[1]
    inflate = count - 1.0
    mean = jnp.sum(ensemble, axis=0, keepdims=True) * (1.0 / count)
    pert = ensemble - mean
    pick = jnp.where(lax.broadcasted_iota(jnp.int32, (lons, obs), 0) == cells, 1.0, 0.0).astype(BF16)
    pert_s = split(pert)
    picked = dot(pert_s[0], pick) + dot(pert_s[1], pick)
    mean_s = split(jnp.broadcast_to(mean, (8, lons)))
    obs_mean = dot(mean_s[0], pick) + dot(mean_s[1], pick)
    root_weight = jnp.sqrt(weights)
    scaled = picked * root_weight
    target = (values - obs_mean) * root_weight
    scaled_s = split(scaled)
    turned_s = (scaled_s[0].T, scaled_s[1].T)
    gram = dot3(turned_s, scaled_s)
    cross = dot3(turned_s, pert_s)
    trace = jnp.sum(jnp.sum(scaled * scaled, axis=0, keepdims=True), axis=1, keepdims=True)
    square = jnp.sum(jnp.sum(gram * gram, axis=0, keepdims=True), axis=1, keepdims=True)
    frob = jnp.sqrt(square + 2.0 * inflate * trace + inflate * inflate * count)
    unit = 1.0 / frob
    a0 = inflate * unit
    p1 = 1.5 - 0.5 * a0
    q2 = a0 * p1 * p1
    p2 = 1.5 - 0.5 * q2
    q3 = q2 * p2 * p2
    p3 = 1.5 - 0.5 * q3
    z0 = p1 * p2 * p3
    diagonal = lax.broadcasted_iota(jnp.int32, (obs, obs), 0) == lax.broadcasted_iota(jnp.int32, (obs, obs), 1)
    eye = jnp.where(diagonal, 1.0, 0.0)
    s = gram * unit
    s_s = split(s)
    s2 = dot3(s_s, s_s)
    t2 = (p1 * p1 - a0 * p1) * eye + (0.25 * a0 - p1) * s + 0.25 * s2
    m2 = dot3(s_s, split(t2))
    f2 = p2 * eye - 0.5 * m2
    e = p1 * t2 - 0.5 * m2
    f2_s = split(f2)
    u = dot3(f2_s, f2_s) - (0.5 * q2) * (f2 + p2 * eye)
    k = dot3(f2_s, split(e))
    r = -0.5 * (dot3(split(u), split(k)) + p3 * e + (p3 * p2) * eye)
    r_s = split(r)
    core_s = split(dot3(r_s, split(cross)))
    target_s = split(target)
    lead = 2.0 * z0 * dot3(target_s, s_s) + dot3(split(dot3(target_s, split(s2))), r_s)
    shift = unit * (z0 * z0 * dot3(target_s, split(cross)) + dot3(split(lead), core_s))
    gain = jnp.sqrt(inflate * unit)
    return (mean + shift[:1]) + (gain * z0) * pert + (gain * unit) * dot3(scaled_s, core_s)


def around(x, shift):
    lons = x.shape[-1]
    return pltpu.roll(x.reshape(-1, lons), shift, 1).reshape(x.shape)


def slope(x):
    return around(x, x.shape[-1] - 1) - around(x, 1)


def flow(x, zonal):
    return x - (HALF_STEP * (zonal + x)) * slope(x)


def kernel(groups, bands, state, zonal, merid, cell, value, weight, out,
           q, u, v, cells, values, weights, low_in, high_in, low_next, high_next, low_out, high_out,
           inner, outer, edge, gathered, result, returned,
           load_sem, halo_send, halo_recv, go_send, go_recv, back_send, back_recv, own_sem, ready, band_ready):
    me = lax.axis_index("member")
    band = lax.axis_index("lat")
    members, rows, levels, lons = state.shape
    halves = lons // LANES
    index, odd = me // 2, me % 2
    my_x, my_y = index // SIDE_Y, index % SIDE_Y
    my_row = jnp.where(odd == 0, 2 + my_y, my_y + 1 - 2 * (my_y % 2) + 4 * (my_y // 2))
    my_level = my_x
    below, above = band > 0, band < bands - 1

    loads = [
        pltpu.make_async_copy(state, q, load_sem.at[0]),
        pltpu.make_async_copy(zonal, u, load_sem.at[1]),
        pltpu.make_async_copy(merid, v, load_sem.at[2]),
        pltpu.make_async_copy(cell.at[my_row], cells, load_sem.at[3]),
        pltpu.make_async_copy(value.at[my_row], values, load_sem.at[4]),
        pltpu.make_async_copy(weight.at[my_row], weights, load_sem.at[5]),
    ]
    for load in loads:
        load.start()

    barrier = pltpu.get_barrier_semaphore()

    @pl.when(below)
    def _():
        pl.semaphore_signal(barrier, inc=1, device_id={"lat": band - 1}, device_id_type=MESH)

    @pl.when(me > 0)
    def _():
        def greet(step, carry):
            pl.semaphore_signal(barrier, inc=1, device_id={"member": lax.rem(me + step, groups)}, device_id_type=MESH)
            return carry

        lax.fori_loop(1, groups, greet, 0)

    pl.semaphore_wait(barrier, groups - 2 + (me == 0).astype(jnp.int32) + above.astype(jnp.int32))

    def to_band(number, src, dst, step):
        return pltpu.make_async_remote_copy(
            src_ref=src, dst_ref=dst, send_sem=halo_send.at[number], recv_sem=halo_recv.at[number],
            device_id={"lat": band + step}, device_id_type=MESH)

    def row_up():
        return to_band(0, state.at[:, rows - 1], low_in, 1)

    def row_down():
        return to_band(1, state.at[:, 0], high_in, -1)

    def next_up():
        return to_band(2, high_out, low_next, 1)

    def next_down():
        return to_band(3, low_out, high_next, -1)

    @pl.when(above)
    def _():
        pl.semaphore_signal(band_ready, inc=1, device_id={"lat": band + 1}, device_id_type=MESH)
        row_up().start()

    @pl.when(me == 0)
    def _():
        def answer(step, carry):
            pl.semaphore_signal(ready, inc=1, device_id={"member": step}, device_id_type=MESH)
            return carry

        lax.fori_loop(1, groups, answer, 0)

    @pl.when(below & (me > 0))
    def _():
        pl.semaphore_wait(band_ready, 1)
        row_down().start()

    for load in loads[:3]:
        load.wait()

    wind_u, wind_v = u[...], HALF_STEP * v[...]

    def put(block, x, place, every):
        for half in range(halves):
            for member in range(members):
                block[pl.ds(place * 8 + half * members + member, levels, stride=8 * every), :] = (
                    x[member, :, half * LANES : (half + 1) * LANES])

    old = q[...]
    mid = flow(old[:, 1:7], wind_u[1:7]) - wind_v[1:7] * (old[:, 2:] - old[:, :6])
    new = flow(mid[:, 1:5], wind_u[2:6]) - wind_v[2:6] * (mid[:, 2:] - mid[:, :4])
    for row in range(4):
        put(inner, new[:, row], row, 4)

    far_x = [(lax.rem(my_x + dx, SIDE_X)) for dx in FAR_X]
    far_y = [(lax.rem(my_y + dy, SIDE_Y)) for dy in FAR_Y]
    mine = pl.ds(pl.multiple_of(me * 8, 8), 8)

    def go(block, tile, peer):
        return pltpu.make_async_remote_copy(
            src_ref=block.at[pl.ds(pl.multiple_of(tile * 8, 8), 8)], dst_ref=gathered.at[mine],
            send_sem=go_send, recv_sem=go_recv, device_id={"member": peer}, device_id_type=MESH)

    for x in far_x:
        for y in far_y:
            tile = x * SIDE_Y + y

            @pl.when((tile > 0) & (2 * tile != me))
            def _():
                go(inner, tile, 2 * tile).start()

    @pl.when(below & (me == 0))
    def _():
        pl.semaphore_wait(band_ready, 1)
        row_down().start()

    first, last = old[:, 0], old[:, 7]

    @pl.when(below)
    def _():
        row_up().wait_recv()

    @pl.when(band == 0)
    def _():
        low_in[...] = jnp.zeros_like(low_in)
        low_next[...] = jnp.zeros_like(low_next)

    row0 = flow(first, wind_u[0]) - wind_v[0] * (old[:, 1] - low_in[...])
    low_out[...] = row0

    @pl.when(below)
    def _():
        next_down().start()

    @pl.when(above)
    def _():
        row_down().wait_recv()

    @pl.when(band == bands - 1)
    def _():
        high_in[...] = jnp.zeros_like(high_in)
        high_next[...] = jnp.zeros_like(high_next)

    row7 = flow(last, wind_u[7]) - wind_v[7] * (high_in[...] - old[:, 6])
    high_out[...] = row7

    @pl.when(above)
    def _():
        next_up().start()

    put(outer, flow(mid[:, 0], wind_u[1]) - wind_v[1] * (mid[:, 1] - row0), 0, 2)
    put(outer, flow(mid[:, 5], wind_u[6]) - wind_v[6] * (row7 - mid[:, 4]), 1, 2)

    def send_odd(block, near, far):
        for x in far_x:
            for slot, y in enumerate((near, far)):
                peer = x * 8 + 2 * y + 1

                @pl.when(peer != me)
                def _():
                    go(block, x * 2 + slot, peer).start()

    send_odd(outer, 0, 3)

    @pl.when(below)
    def _():
        next_up().wait_recv()

    @pl.when(above)
    def _():
        next_down().wait_recv()

    put(edge, flow(row0, wind_u[0]) - wind_v[0] * (mid[:, 0] - low_next[...]), 0, 2)
    put(edge, flow(row7, wind_u[7]) - wind_v[7] * (high_next[...] - mid[:, 5]), 1, 2)
    send_odd(edge, 1, 2)

    def keep(block, tile):
        return pltpu.make_async_copy(block.at[pl.ds(pl.multiple_of(tile * 8, 8), 8)], gathered.at[mine], own_sem.at[0])

    @pl.when(odd == 0)
    def _():
        keep(inner, index).start()

    @pl.when((odd == 1) & ((my_y == 0) | (my_y == 3)))
    def _():
        keep(outer, my_x * 2 + my_y // 3).start()

    @pl.when((odd == 1) & ((my_y == 1) | (my_y == 2)))
    def _():
        keep(edge, my_x * 2 + my_y // 2).start()

    @pl.when(me > 0)
    def _():
        pl.semaphore_wait(ready, 1)
        go(inner, 0, 0).start()

    keep(inner, index).wait()
    for load in loads[3:]:
        load.wait()
    others = pl.ds(0, (groups - 1) * 8)
    pltpu.make_async_copy(gathered.at[others], gathered.at[others], go_recv).wait()

    ensemble = jnp.concatenate(
        [jnp.concatenate(
            [gathered[pl.ds(half * members + member, groups, stride=8), :] for member in range(members)], axis=0)
         for half in range(halves)], axis=1)
    analysed = analyse(
        ensemble, cells[pl.ds(my_level, 1), :], values[pl.ds(my_level, 1), :], weights[pl.ds(my_level, 1), :])
    for half in range(halves):
        for member in range(members):
            result[pl.ds(half * members + member, groups, stride=8), :] = (
                analysed[member * groups : (member + 1) * groups, half * LANES : (half + 1) * LANES])

    def give(peer):
        return pltpu.make_async_remote_copy(
            src_ref=result.at[pl.ds(pl.multiple_of(peer * 8, 8), 8)], dst_ref=returned.at[mine],
            send_sem=back_send, recv_sem=back_recv, device_id={"member": peer}, device_id_type=MESH)

    for x in far_x:
        for y in far_y:
            for core in range(2):
                peer = x * 8 + 2 * y + core
                if (x is far_x[-1]) and (y is far_y[-1]):

                    @pl.when(odd != core)
                    def _():
                        give(peer).start()
                else:
                    give(peer).start()

    own = pltpu.make_async_copy(result.at[mine], returned.at[mine], own_sem.at[1])
    own.start()
    own.wait()
    pltpu.make_async_copy(returned.at[others], returned.at[others], back_recv).wait()

    for row, place, core in ((2, 0, 0), (3, 1, 0), (4, 2, 0), (5, 3, 0), (1, 0, 1), (0, 1, 1), (7, 2, 1), (6, 3, 1)):
        for half in range(halves):
            for member in range(members):
                start = (2 * place + core) * 8 + half * members + member
                out[member, row, :, half * LANES : (half + 1) * LANES] = returned[pl.ds(start, levels, stride=64), :]

    @pl.when(below)
    def _():
        row_down().wait_send()
        next_down().wait_send()

    @pl.when(above)
    def _():
        row_up().wait_send()
        next_up().wait_send()

    pltpu.make_async_copy(gathered.at[others], gathered.at[others], go_send).wait()
    pltpu.make_async_copy(returned.at[others], returned.at[others], back_send).wait()


def solution(mesh):
    groups, bands = mesh.shape["member"], mesh.shape["lat"]
    assert groups == 2 * SIDE_X * SIDE_Y

    def body(state, zonal, merid, cell, value, weight):
        members, rows, levels, lons = state.shape
        obs = cell.shape[-1]
        halo = pltpu.VMEM((members, levels, lons), F32)
        tiles = groups * 8
        return pl.pallas_call(
            lambda *refs: kernel(groups, bands, *refs),
            out_shape=pltpu.VMEM(state.shape, F32),
            in_specs=[pl.BlockSpec(memory_space=pltpu.HBM)] * 6,
            out_specs=pl.BlockSpec(memory_space=pltpu.VMEM),
            scratch_shapes=[
                pltpu.VMEM(state.shape, F32),
                pltpu.VMEM(zonal.shape, F32),
                pltpu.VMEM(merid.shape, F32),
                pltpu.VMEM((levels, obs), jnp.int32),
                pltpu.VMEM((levels, obs), F32),
                pltpu.VMEM((levels, obs), F32),
                halo, halo, halo, halo, halo, halo,
                pltpu.VMEM((tiles // 2, LANES), F32),
                pltpu.VMEM((tiles // 4, LANES), F32),
                pltpu.VMEM((tiles // 4, LANES), F32),
                pltpu.VMEM((tiles, LANES), F32),
                pltpu.VMEM((tiles, LANES), F32),
                pltpu.VMEM((tiles, LANES), F32),
                pltpu.SemaphoreType.DMA((6,)),
                pltpu.SemaphoreType.DMA((4,)),
                pltpu.SemaphoreType.DMA((4,)),
                pltpu.SemaphoreType.DMA,
                pltpu.SemaphoreType.DMA,
                pltpu.SemaphoreType.DMA,
                pltpu.SemaphoreType.DMA,
                pltpu.SemaphoreType.DMA((2,)),
                pltpu.SemaphoreType.REGULAR,
                pltpu.SemaphoreType.REGULAR,
            ],
            compiler_params=pltpu.CompilerParams(collective_id=0, has_side_effects=True, vmem_limit_bytes=56 * 1024 * 1024),
        )(state, zonal, merid, cell, value, weight)

    in_specs = (P("member", "lat", None, None),) + (P("lat", None, None),) * 5
    return jax.shard_map(body, mesh=mesh, in_specs=in_specs, out_specs=P("member", "lat", None, None), check_vma=False)
```

```python
import math

import jax
import jax.numpy as jnp
from jax import lax
from jax.experimental import pallas as pl
from jax.experimental.pallas import tpu as pltpu
from jax.sharding import PartitionSpec as P

MESH = pl.DeviceIdType.MESH
F32 = jnp.float32
BF16 = jnp.bfloat16
HALF_STEP = 0.15
LANES = 128
SIDE_X, SIDE_Y = 8, 4
FAR_X = (4, 5, 3, 6, 2, 7, 1, 0)
FAR_Y = (2, 1, 3, 0)


def split(x):
    high = x.astype(BF16)
    low = (x - high.astype(F32)).astype(BF16)
    return high, low


def dot(a, b):
    return lax.dot_general(a, b, (((1,), (0,)), ((), ())), preferred_element_type=F32)


def dot3(a, b):
    return dot(a[0], b[0]) + (dot(a[0], b[1]) + dot(a[1], b[0]))


def analyse(ensemble, cells, values, weights):
    count, lons = ensemble.shape
    obs = cells.shape[1]
    inflate = count - 1.0
    mean = jnp.sum(ensemble, axis=0, keepdims=True) * (1.0 / count)
    pert = ensemble - mean
    pick = jnp.where(lax.broadcasted_iota(jnp.int32, (lons, obs), 0) == cells, 1.0, 0.0).astype(BF16)
    pert_s = split(pert)
    picked = dot(pert_s[0], pick) + dot(pert_s[1], pick)
    mean_s = split(jnp.broadcast_to(mean, (8, lons)))
    obs_mean = dot(mean_s[0], pick) + dot(mean_s[1], pick)
    root_weight = jnp.sqrt(weights)
    scaled = picked * root_weight
    target = (values - obs_mean) * root_weight
    scaled_s = split(scaled)
    turned_s = (scaled_s[0].T, scaled_s[1].T)
    gram = dot3(turned_s, scaled_s)
    cross = dot3(turned_s, pert_s)
    trace = jnp.sum(jnp.sum(scaled * scaled, axis=0, keepdims=True), axis=1, keepdims=True)
    square = jnp.sum(jnp.sum(gram * gram, axis=0, keepdims=True), axis=1, keepdims=True)
    frob = jnp.sqrt(square + 2.0 * inflate * trace + inflate * inflate * count)
    unit = 1.0 / frob
    a0 = inflate * unit
    p1 = 1.5 - 0.5 * a0
    q2 = a0 * p1 * p1
    p2 = 1.5 - 0.5 * q2
    q3 = q2 * p2 * p2
    p3 = 1.5 - 0.5 * q3
    z0 = p1 * p2 * p3
    diagonal = lax.broadcasted_iota(jnp.int32, (obs, obs), 0) == lax.broadcasted_iota(jnp.int32, (obs, obs), 1)
    eye = jnp.where(diagonal, 1.0, 0.0)
    s = gram * unit
    s_s = split(s)
    s2 = dot3(s_s, s_s)
    t2 = (p1 * p1 - a0 * p1) * eye + (0.25 * a0 - p1) * s + 0.25 * s2
    m2 = dot3(s_s, split(t2))
    f2 = p2 * eye - 0.5 * m2
    e = p1 * t2 - 0.5 * m2
    f2_s = split(f2)
    u = dot3(f2_s, f2_s) - (0.5 * q2) * (f2 + p2 * eye)
    k = dot3(f2_s, split(e))
    r = -0.5 * (dot3(split(u), split(k)) + p3 * e + (p3 * p2) * eye)
    r_s = split(r)
    core_s = split(dot3(r_s, split(cross)))
    target_s = split(target)
    lead = 2.0 * z0 * dot3(target_s, s_s) + dot3(split(dot3(target_s, split(s2))), r_s)
    shift = unit * (z0 * z0 * dot3(target_s, split(cross)) + dot3(split(lead), core_s))
    gain = jnp.sqrt(inflate * unit)
    return (mean + shift[:1]) + (gain * z0) * pert + (gain * unit) * dot3(scaled_s, core_s)


def around(x, shift):
    lons = x.shape[-1]
    return pltpu.roll(x.reshape(-1, lons), shift, 1).reshape(x.shape)


def slope(x):
    return around(x, x.shape[-1] - 1) - around(x, 1)


def flow(x, zonal):
    return x - (HALF_STEP * (zonal + x)) * slope(x)


def kernel(groups, bands, state, zonal, merid, cell, value, weight, out,
           q, u, v, cells, values, weights, low_in, high_in, low_out, high_out,
           inner, outer, edge, gathered, result, returned,
           load_sem, halo_send, halo_recv, go_send, go_recv, back_send, back_recv, own_sem, ready, band_ready):
    me = lax.axis_index("member")
    band = lax.axis_index("lat")
    members, rows, levels, lons = state.shape
    halves = lons // LANES
    index, odd = me // 2, me % 2
    my_x, my_y = index // SIDE_Y, index % SIDE_Y
    my_row = jnp.where(odd == 0, 2 + my_y, my_y + 4 * (my_y // 2))
    my_level = my_x
    below, above = band > 0, band < bands - 1

    loads = [
        pltpu.make_async_copy(state, q, load_sem.at[0]),
        pltpu.make_async_copy(zonal, u, load_sem.at[1]),
        pltpu.make_async_copy(merid, v, load_sem.at[2]),
        pltpu.make_async_copy(cell.at[my_row], cells, load_sem.at[3]),
        pltpu.make_async_copy(value.at[my_row], values, load_sem.at[4]),
        pltpu.make_async_copy(weight.at[my_row], weights, load_sem.at[5]),
    ]
    for load in loads:
        load.start()

    late = (me == 0) & (band == 0)
    barrier = pltpu.get_barrier_semaphore()

    @pl.when(below)
    def _():
        pl.semaphore_signal(barrier, inc=1, device_id={"lat": band - 1}, device_id_type=MESH)

    @pl.when(above & jnp.logical_not(late))
    def _():
        pl.semaphore_signal(barrier, inc=1, device_id={"lat": band + 1}, device_id_type=MESH)

    @pl.when(jnp.logical_not(late))
    def _():
        def greet(step, carry):
            pl.semaphore_signal(barrier, inc=1, device_id={"member": lax.rem(me + step, groups)}, device_id_type=MESH)
            return carry

        lax.fori_loop(1, groups, greet, 0)

    for load in loads[:3]:
        load.wait()

    wind_u, wind_v = u[...], HALF_STEP * v[...]
    old = q[...]
    first, last = old[:, 0], old[:, 7]

    low_out[:members] = first
    low_out[members : 2 * members] = flow(first, wind_u[0]) - wind_v[0] * old[:, 1]
    low_out[2 * members] = wind_v[0]
    high_out[:members] = last
    high_out[members : 2 * members] = flow(last, wind_u[7]) + wind_v[7] * old[:, 6]
    high_out[2 * members] = wind_v[7]

    def to_low():
        return pltpu.make_async_remote_copy(
            src_ref=low_out, dst_ref=high_in, send_sem=halo_send.at[0], recv_sem=halo_recv.at[0],
            device_id={"lat": band - 1}, device_id_type=MESH)

    def to_high():
        return pltpu.make_async_remote_copy(
            src_ref=high_out, dst_ref=low_in, send_sem=halo_send.at[1], recv_sem=halo_recv.at[1],
            device_id={"lat": band + 1}, device_id_type=MESH)

    def put(block, x, place, every):
        for half in range(halves):
            for member in range(members):
                block[pl.ds(place * 8 + half * members + member, levels, stride=8 * every), :] = (
                    x[member, :, half * LANES : (half + 1) * LANES])

    mid = flow(old[:, 1:7], wind_u[1:7]) - wind_v[1:7] * (old[:, 2:] - old[:, :6])
    new = flow(mid[:, 1:5], wind_u[2:6]) - wind_v[2:6] * (mid[:, 2:] - mid[:, :4])
    for row in range(4):
        put(inner, new[:, row], row, 4)

    after_late = ((me > 0) & (band == 0)) | ((me == 0) & (band == 1))
    pl.semaphore_wait(
        barrier,
        groups - 1 + below.astype(jnp.int32) + above.astype(jnp.int32) - after_late.astype(jnp.int32))

    @pl.when(late)
    def _():
        pl.semaphore_signal(band_ready, inc=1, device_id={"lat": band + 1}, device_id_type=MESH)

        def answer(step, carry):
            pl.semaphore_signal(ready, inc=1, device_id={"member": step}, device_id_type=MESH)
            return carry

        lax.fori_loop(1, groups, answer, 0)

    @pl.when(above)
    def _():
        to_high().start()

    @pl.when(below & jnp.logical_not(after_late))
    def _():
        to_low().start()

    far_x = [(lax.rem(my_x + dx, SIDE_X)) for dx in FAR_X]
    far_y = [(lax.rem(my_y + dy, SIDE_Y)) for dy in FAR_Y]
    mine = pl.ds(pl.multiple_of(me * 8, 8), 8)

    def go(block, tile, peer):
        return pltpu.make_async_remote_copy(
            src_ref=block.at[pl.ds(pl.multiple_of(tile * 8, 8), 8)], dst_ref=gathered.at[mine],
            send_sem=go_send, recv_sem=go_recv, device_id={"member": peer}, device_id_type=MESH)

    for x in far_x:
        for y in far_y:
            tile = x * SIDE_Y + y

            @pl.when(((tile > 0) | (band > 0)) & (2 * tile != me))
            def _():
                go(inner, tile, 2 * tile).start()

    @pl.when(below & after_late)
    def _():
        pl.semaphore_wait(band_ready, 1)
        to_low().start()

    def send_odd(block, near, far):
        for x in far_x:
            for slot, y in enumerate((near, far)):
                peer = x * 8 + 2 * y + 1

                @pl.when(peer != me)
                def _():
                    go(block, x * 2 + slot, peer).start()

    @pl.when(below)
    def _():
        to_high().wait_recv()

    @pl.when(band == 0)
    def _():
        low_in[...] = jnp.zeros_like(low_in)

    row0 = flow(first, wind_u[0]) - wind_v[0] * (old[:, 1] - low_in[:members])
    before = low_in[members : 2 * members] - low_in[2 * members] * first
    put(outer, flow(row0, wind_u[0]) - wind_v[0] * (mid[:, 0] - before), 0, 2)
    put(outer, flow(mid[:, 0], wind_u[1]) - wind_v[1] * (mid[:, 1] - row0), 1, 2)
    send_odd(outer, 0, 1)

    @pl.when(above)
    def _():
        to_low().wait_recv()

    @pl.when(band == bands - 1)
    def _():
        high_in[...] = jnp.zeros_like(high_in)

    row7 = flow(last, wind_u[7]) - wind_v[7] * (high_in[:members] - old[:, 6])
    after = high_in[members : 2 * members] + high_in[2 * members] * last
    put(edge, flow(mid[:, 5], wind_u[6]) - wind_v[6] * (row7 - mid[:, 4]), 0, 2)
    put(edge, flow(row7, wind_u[7]) - wind_v[7] * (after - mid[:, 5]), 1, 2)
    send_odd(edge, 2, 3)

    def keep(block, tile):
        return pltpu.make_async_copy(block.at[pl.ds(pl.multiple_of(tile * 8, 8), 8)], gathered.at[mine], own_sem.at[0])

    @pl.when(odd == 0)
    def _():
        keep(inner, index).start()

    @pl.when((odd == 1) & (my_y < 2))
    def _():
        keep(outer, my_x * 2 + my_y).start()

    @pl.when((odd == 1) & (my_y >= 2))
    def _():
        keep(edge, my_x * 2 + my_y - 2).start()

    @pl.when((me > 0) & (band == 0))
    def _():
        pl.semaphore_wait(ready, 1)
        go(inner, 0, 0).start()

    keep(inner, index).wait()
    for load in loads[3:]:
        load.wait()
    others = pl.ds(0, (groups - 1) * 8)
    pltpu.make_async_copy(gathered.at[others], gathered.at[others], go_recv).wait()

    ensemble = jnp.concatenate(
        [jnp.concatenate(
            [gathered[pl.ds(half * members + member, groups, stride=8), :] for member in range(members)], axis=0)
         for half in range(halves)], axis=1)
    analysed = analyse(
        ensemble, cells[pl.ds(my_level, 1), :], values[pl.ds(my_level, 1), :], weights[pl.ds(my_level, 1), :])
    for half in range(halves):
        for member in range(members):
            result[pl.ds(half * members + member, groups, stride=8), :] = (
                analysed[member * groups : (member + 1) * groups, half * LANES : (half + 1) * LANES])

    def give(peer):
        return pltpu.make_async_remote_copy(
            src_ref=result.at[pl.ds(pl.multiple_of(peer * 8, 8), 8)], dst_ref=returned.at[mine],
            send_sem=back_send, recv_sem=back_recv, device_id={"member": peer}, device_id_type=MESH)

    for x in far_x:
        for y in far_y:
            for core in range(2):
                peer = x * 8 + 2 * y + core
                if (x is far_x[-1]) and (y is far_y[-1]):

                    @pl.when(odd != core)
                    def _():
                        give(peer).start()
                else:
                    give(peer).start()

    own = pltpu.make_async_copy(result.at[mine], returned.at[mine], own_sem.at[1])
    own.start()
    own.wait()
    pltpu.make_async_copy(returned.at[others], returned.at[others], back_recv).wait()

    for row, place, core in ((2, 0, 0), (3, 1, 0), (4, 2, 0), (5, 3, 0), (0, 0, 1), (1, 1, 1), (6, 2, 1), (7, 3, 1)):
        for half in range(halves):
            for member in range(members):
                start = (2 * place + core) * 8 + half * members + member
                out[member, row, :, half * LANES : (half + 1) * LANES] = returned[pl.ds(start, levels, stride=64), :]

    @pl.when(below)
    def _():
        to_low().wait_send()

    @pl.when(above)
    def _():
        to_high().wait_send()

    pltpu.make_async_copy(gathered.at[others], gathered.at[others], go_send).wait()
    pltpu.make_async_copy(returned.at[others], returned.at[others], back_send).wait()


def solution(mesh):
    groups, bands = mesh.shape["member"], mesh.shape["lat"]
    assert groups == 2 * SIDE_X * SIDE_Y

    def body(state, zonal, merid, cell, value, weight):
        members, rows, levels, lons = state.shape
        obs = cell.shape[-1]
        halo = pltpu.VMEM((2 * members + 1, levels, lons), F32)
        tiles = groups * 8
        return pl.pallas_call(
            lambda *refs: kernel(groups, bands, *refs),
            out_shape=pltpu.VMEM(state.shape, F32),
            in_specs=[pl.BlockSpec(memory_space=pltpu.HBM)] * 6,
            out_specs=pl.BlockSpec(memory_space=pltpu.VMEM),
            scratch_shapes=[
                pltpu.VMEM(state.shape, F32),
                pltpu.VMEM(zonal.shape, F32),
                pltpu.VMEM(merid.shape, F32),
                pltpu.VMEM((levels, obs), jnp.int32),
                pltpu.VMEM((levels, obs), F32),
                pltpu.VMEM((levels, obs), F32),
                halo, halo, halo, halo,
                pltpu.VMEM((tiles // 2, LANES), F32),
                pltpu.VMEM((tiles // 4, LANES), F32),
                pltpu.VMEM((tiles // 4, LANES), F32),
                pltpu.VMEM((tiles, LANES), F32),
                pltpu.VMEM((tiles, LANES), F32),
                pltpu.VMEM((tiles, LANES), F32),
                pltpu.SemaphoreType.DMA((6,)),
                pltpu.SemaphoreType.DMA((2,)),
                pltpu.SemaphoreType.DMA((2,)),
                pltpu.SemaphoreType.DMA,
                pltpu.SemaphoreType.DMA,
                pltpu.SemaphoreType.DMA,
                pltpu.SemaphoreType.DMA,
                pltpu.SemaphoreType.DMA((2,)),
                pltpu.SemaphoreType.REGULAR,
                pltpu.SemaphoreType.REGULAR,
            ],
            compiler_params=pltpu.CompilerParams(collective_id=0, has_side_effects=True, vmem_limit_bytes=56 * 1024 * 1024),
        )(state, zonal, merid, cell, value, weight)

    in_specs = (P("member", "lat", None, None),) + (P("lat", None, None),) * 5
    return jax.shard_map(body, mesh=mesh, in_specs=in_specs, out_specs=P("member", "lat", None, None), check_vma=False)
```

```python
import math

import jax
import jax.numpy as jnp
from jax import lax
from jax.experimental import pallas as pl
from jax.experimental.pallas import tpu as pltpu
from jax.sharding import PartitionSpec as P

MESH = pl.DeviceIdType.MESH
F32 = jnp.float32
BF16 = jnp.bfloat16
HALF_STEP = 0.15
LANES = 128
SIDE_X, SIDE_Y = 8, 4
FAR_X = (4, 5, 3, 6, 2, 7, 1, 0)
FAR_Y = (2, 1, 3, 0)


def split(x):
    high = x.astype(BF16)
    low = (x - high.astype(F32)).astype(BF16)
    return high, low


def dot(a, b):
    return lax.dot_general(a, b, (((1,), (0,)), ((), ())), preferred_element_type=F32)


def dot3(a, b):
    return dot(a[0], b[0]) + (dot(a[0], b[1]) + dot(a[1], b[0]))


def analyse(ensemble, cells, values, weights):
    count, lons = ensemble.shape
    obs = cells.shape[1]
    inflate = count - 1.0
    mean = jnp.sum(ensemble, axis=0, keepdims=True) * (1.0 / count)
    pert = ensemble - mean
    pick = jnp.where(lax.broadcasted_iota(jnp.int32, (lons, obs), 0) == cells, 1.0, 0.0).astype(BF16)
    pert_s = split(pert)
    picked = dot(pert_s[0], pick) + dot(pert_s[1], pick)
    mean_s = split(jnp.broadcast_to(mean, (8, lons)))
    obs_mean = dot(mean_s[0], pick) + dot(mean_s[1], pick)
    root_weight = jnp.sqrt(weights)
    scaled = picked * root_weight
    target = (values - obs_mean) * root_weight
    scaled_s = split(scaled)
    turned_s = (scaled_s[0].T, scaled_s[1].T)
    gram = dot3(turned_s, scaled_s)
    gram_s = split(gram)
    twice = dot3(gram_s, gram_s)
    cross = dot3(turned_s, pert_s)
    trace = jnp.sum(jnp.sum(scaled * scaled, axis=0, keepdims=True), axis=1, keepdims=True)
    square = jnp.sum(jnp.sum(gram * gram, axis=0, keepdims=True), axis=1, keepdims=True)
    frob = jnp.sqrt(square + 2.0 * inflate * trace + inflate * inflate * count)
    unit = 1.0 / frob
    a0 = inflate * unit
    p1 = 1.5 - 0.5 * a0
    q2 = a0 * p1 * p1
    p2 = 1.5 - 0.5 * q2
    q3 = q2 * p2 * p2
    p3 = 1.5 - 0.5 * q3
    z0 = p1 * p2 * p3
    diagonal = lax.broadcasted_iota(jnp.int32, (obs, obs), 0) == lax.broadcasted_iota(jnp.int32, (obs, obs), 1)
    eye = jnp.where(diagonal, 1.0, 0.0)
    s = gram * unit
    s_s = split(s)
    s2 = (twice * unit) * unit
    t2 = (p1 * p1 - a0 * p1) * eye + (0.25 * a0 - p1) * s + 0.25 * s2
    m2 = dot3(s_s, split(t2))
    f2 = p2 * eye - 0.5 * m2
    e = p1 * t2 - 0.5 * m2
    f2_s = split(f2)
    u = dot3(f2_s, f2_s) - (0.5 * q2) * (f2 + p2 * eye)
    k = dot3(f2_s, split(e))
    r = -0.5 * (dot3(split(u), split(k)) + p3 * e + (p3 * p2) * eye)
    r_s = split(r)
    core_s = split(dot3(r_s, split(cross)))
    target_s = split(target)
    lead = 2.0 * z0 * dot3(target_s, s_s) + dot3(split(dot3(target_s, split(s2))), r_s)
    shift = unit * (z0 * z0 * dot3(target_s, split(cross)) + dot3(split(lead), core_s))
    gain = jnp.sqrt(inflate * unit)
    return (mean + shift[:1]) + (gain * z0) * pert + (gain * unit) * dot3(scaled_s, core_s)


def around(x, shift):
    lons = x.shape[-1]
    return pltpu.roll(x.reshape(-1, lons), shift, 1).reshape(x.shape)


def slope(x):
    return around(x, x.shape[-1] - 1) - around(x, 1)


def flow(x, zonal):
    return x - (HALF_STEP * (zonal + x)) * slope(x)


def kernel(groups, bands, state, zonal, merid, cell, value, weight, out,
           q, u, v, cells, values, weights, low_in, high_in, low_out, high_out,
           inner, outer, edge, gathered, result, returned,
           load_sem, halo_send, halo_recv, go_send, go_recv, back_send, back_recv, own_sem, ready, band_ready):
    me = lax.axis_index("member")
    band = lax.axis_index("lat")
    members, rows, levels, lons = state.shape
    halves = lons // LANES
    index, odd = me // 2, me % 2
    my_x, my_y = index // SIDE_Y, index % SIDE_Y
    slot = lax.rem(my_y + 2 * (my_x % 2), SIDE_Y)
    my_row = jnp.where(odd == 0, 2 + my_y, jnp.where(slot < 2, 1 + 5 * slot, 7 * (slot - 2)))
    home = my_x * 8 + jnp.where(odd == 0, 2 * my_y, 2 * slot + 1)
    my_level = my_x
    below, above = band > 0, band < bands - 1

    loads = [
        pltpu.make_async_copy(state, q, load_sem.at[0]),
        pltpu.make_async_copy(zonal, u, load_sem.at[1]),
        pltpu.make_async_copy(merid, v, load_sem.at[2]),
        pltpu.make_async_copy(cell.at[my_row], cells, load_sem.at[3]),
        pltpu.make_async_copy(value.at[my_row], values, load_sem.at[4]),
        pltpu.make_async_copy(weight.at[my_row], weights, load_sem.at[5]),
    ]
    for load in loads:
        load.start()

    late = (me == 0) & (band == 0)
    barrier = pltpu.get_barrier_semaphore()

    @pl.when(below)
    def _():
        pl.semaphore_signal(barrier, inc=1, device_id={"lat": band - 1}, device_id_type=MESH)

    @pl.when(above & jnp.logical_not(late))
    def _():
        pl.semaphore_signal(barrier, inc=1, device_id={"lat": band + 1}, device_id_type=MESH)

    @pl.when(jnp.logical_not(late))
    def _():
        def greet(step, carry):
            peer = me + 1 + step
            pl.semaphore_signal(barrier, inc=1, device_id={"member": lax.rem(peer, groups)}, device_id_type=MESH)
            return carry

        lax.fori_loop(0, groups - 1, greet, 0)

    for load in loads[:3]:
        load.wait()

    wind_u, wind_v = u[...], HALF_STEP * v[...]
    old = q[...]
    first, last = old[:, 0], old[:, 7]

    low_out[:members] = first
    low_out[members : 2 * members] = flow(first, wind_u[0]) - wind_v[0] * old[:, 1]
    low_out[2 * members] = wind_v[0]
    high_out[:members] = last
    high_out[members : 2 * members] = flow(last, wind_u[7]) + wind_v[7] * old[:, 6]
    high_out[2 * members] = wind_v[7]

    raw, rest = pl.ds(0, members), pl.ds(members, members + 1)

    def to_low(number, part):
        return pltpu.make_async_remote_copy(
            src_ref=low_out.at[part], dst_ref=high_in.at[part], send_sem=halo_send.at[number], recv_sem=halo_recv.at[number],
            device_id={"lat": band - 1}, device_id_type=MESH)

    def to_high(number, part):
        return pltpu.make_async_remote_copy(
            src_ref=high_out.at[part], dst_ref=low_in.at[part], send_sem=halo_send.at[number], recv_sem=halo_recv.at[number],
            device_id={"lat": band + 1}, device_id_type=MESH)

    def put(block, x, place, every):
        for half in range(halves):
            for member in range(members):
                block[pl.ds(place * 8 + half * members + member, levels, stride=8 * every), :] = (
                    x[member, :, half * LANES : (half + 1) * LANES])

    mid = flow(old[:, 1:7], wind_u[1:7]) - wind_v[1:7] * (old[:, 2:] - old[:, :6])
    new = flow(mid[:, 1:5], wind_u[2:6]) - wind_v[2:6] * (mid[:, 2:] - mid[:, :4])
    for row in range(4):
        put(inner, new[:, row], row, 4)

    after_late = ((me > 0) & (band == 0)) | ((me == 0) & (band == 1))
    pl.semaphore_wait(
        barrier,
        groups - 1 + below.astype(jnp.int32) + above.astype(jnp.int32) - after_late.astype(jnp.int32))

    @pl.when(late)
    def _():
        pl.semaphore_signal(band_ready, inc=1, device_id={"lat": band + 1}, device_id_type=MESH)

        def answer(step, carry):
            pl.semaphore_signal(ready, inc=1, device_id={"member": step}, device_id_type=MESH)
            return carry

        lax.fori_loop(1, groups, answer, 0)

    for number, part in ((0, raw), (2, rest)):

        @pl.when(above)
        def _():
            to_high(number, part).start()

        @pl.when(below & jnp.logical_not(after_late))
        def _():
            to_low(number + 1, part).start()

    far_x = [(lax.rem(my_x + dx, SIDE_X)) for dx in FAR_X]
    turned_y = [[2 * lax.rem(slot + 2 * (x % 2), SIDE_Y) for slot in range(4)] for x in far_x]
    far_y = [(lax.rem(my_y + dy, SIDE_Y)) for dy in FAR_Y]
    mine = pl.ds(pl.multiple_of(me * 8, 8), 8)

    def go(block, tile, peer):
        return pltpu.make_async_remote_copy(
            src_ref=block.at[pl.ds(pl.multiple_of(tile * 8, 8), 8)], dst_ref=gathered.at[mine],
            send_sem=go_send, recv_sem=go_recv, device_id={"member": peer}, device_id_type=MESH)

    for x in far_x:
        for y in far_y:
            tile = x * SIDE_Y + y

            @pl.when(((tile > 0) | (band > 0)) & (2 * tile != me))
            def _():
                go(inner, tile, 2 * tile).start()

    @pl.when(below & after_late)
    def _():
        pl.semaphore_wait(band_ready, 1)
        to_low(1, raw).start()
        to_low(3, rest).start()

    def send_outer(block, first_slot):
        for x, turned in zip(far_x, turned_y):
            for row in range(2):
                peer = x * 8 + (turned[first_slot + row] + 1)

                @pl.when(peer != me)
                def _():
                    go(block, x * 2 + row, peer).start()

    @pl.when(below)
    def _():
        to_high(0, raw).wait_recv()

    @pl.when(band == 0)
    def _():
        low_in[...] = jnp.zeros_like(low_in)

    @pl.when(above)
    def _():
        to_low(1, raw).wait_recv()

    @pl.when(band == bands - 1)
    def _():
        high_in[...] = jnp.zeros_like(high_in)

    row0 = flow(first, wind_u[0]) - wind_v[0] * (old[:, 1] - low_in[:members])
    row7 = flow(last, wind_u[7]) - wind_v[7] * (high_in[:members] - old[:, 6])
    put(outer, flow(mid[:, 0], wind_u[1]) - wind_v[1] * (mid[:, 1] - row0), 0, 2)
    put(outer, flow(mid[:, 5], wind_u[6]) - wind_v[6] * (row7 - mid[:, 4]), 1, 2)
    send_outer(outer, 0)

    @pl.when(below)
    def _():
        to_high(2, rest).wait_recv()

    @pl.when(above)
    def _():
        to_low(3, rest).wait_recv()

    before = low_in[members : 2 * members] - low_in[2 * members] * first
    after = high_in[members : 2 * members] + high_in[2 * members] * last
    put(edge, flow(row0, wind_u[0]) - wind_v[0] * (mid[:, 0] - before), 0, 2)
    put(edge, flow(row7, wind_u[7]) - wind_v[7] * (after - mid[:, 5]), 1, 2)
    send_outer(edge, 2)

    def keep(block, tile):
        return pltpu.make_async_copy(block.at[pl.ds(pl.multiple_of(tile * 8, 8), 8)], gathered.at[mine], own_sem.at[0])

    @pl.when(odd == 0)
    def _():
        keep(inner, index).start()

    @pl.when((odd == 1) & (slot < 2))
    def _():
        keep(outer, my_x * 2 + slot).start()

    @pl.when((odd == 1) & (slot >= 2))
    def _():
        keep(edge, my_x * 2 + slot - 2).start()

    @pl.when((me > 0) & (band == 0))
    def _():
        pl.semaphore_wait(ready, 1)
        go(inner, 0, 0).start()

    keep(inner, index).wait()
    for load in loads[3:]:
        load.wait()
    others = pl.ds(0, (groups - 1) * 8)
    pltpu.make_async_copy(gathered.at[others], gathered.at[others], go_recv).wait()

    ensemble = jnp.concatenate(
        [jnp.concatenate(
            [gathered[pl.ds(half * members + member, groups, stride=8), :] for member in range(members)], axis=0)
         for half in range(halves)], axis=1)
    analysed = analyse(
        ensemble, cells[pl.ds(my_level, 1), :], values[pl.ds(my_level, 1), :], weights[pl.ds(my_level, 1), :])
    for half in range(halves):
        for member in range(members):
            result[pl.ds(half * members + member, groups, stride=8), :] = (
                analysed[member * groups : (member + 1) * groups, half * LANES : (half + 1) * LANES])

    there = pl.ds(pl.multiple_of(home * 8, 8), 8)

    def give(peer):
        return pltpu.make_async_remote_copy(
            src_ref=result.at[pl.ds(pl.multiple_of(peer * 8, 8), 8)], dst_ref=returned.at[there],
            send_sem=back_send, recv_sem=back_recv, device_id={"member": peer}, device_id_type=MESH)

    for x in far_x:
        for y in far_y:
            for core in range(2):
                peer = x * 8 + 2 * y + core
                if (x is far_x[-1]) and (y is far_y[-1]):

                    @pl.when(odd != core)
                    def _():
                        give(peer).start()
                else:
                    give(peer).start()

    own = pltpu.make_async_copy(result.at[mine], returned.at[there], own_sem.at[1])
    own.start()
    own.wait()
    pltpu.make_async_copy(returned.at[others], returned.at[others], back_recv).wait()

    for row, place, core in ((2, 0, 0), (3, 1, 0), (4, 2, 0), (5, 3, 0), (1, 0, 1), (6, 1, 1), (0, 2, 1), (7, 3, 1)):
        for half in range(halves):
            for member in range(members):
                start = (2 * place + core) * 8 + half * members + member
                out[member, row, :, half * LANES : (half + 1) * LANES] = returned[pl.ds(start, levels, stride=64), :]

    @pl.when(below)
    def _():
        to_low(1, raw).wait_send()
        to_low(3, rest).wait_send()

    @pl.when(above)
    def _():
        to_high(0, raw).wait_send()
        to_high(2, rest).wait_send()

    pltpu.make_async_copy(gathered.at[others], gathered.at[others], go_send).wait()
    pltpu.make_async_copy(returned.at[others], returned.at[others], back_send).wait()


def solution(mesh):
    groups, bands = mesh.shape["member"], mesh.shape["lat"]
    assert groups == 2 * SIDE_X * SIDE_Y

    def body(state, zonal, merid, cell, value, weight):
        members, rows, levels, lons = state.shape
        obs = cell.shape[-1]
        halo = pltpu.VMEM((2 * members + 1, levels, lons), F32)
        tiles = groups * 8
        return pl.pallas_call(
            lambda *refs: kernel(groups, bands, *refs),
            out_shape=pltpu.VMEM(state.shape, F32),
            in_specs=[pl.BlockSpec(memory_space=pltpu.HBM)] * 6,
            out_specs=pl.BlockSpec(memory_space=pltpu.VMEM),
            scratch_shapes=[
                pltpu.VMEM(state.shape, F32),
                pltpu.VMEM(zonal.shape, F32),
                pltpu.VMEM(merid.shape, F32),
                pltpu.VMEM((levels, obs), jnp.int32),
                pltpu.VMEM((levels, obs), F32),
                pltpu.VMEM((levels, obs), F32),
                halo, halo, halo, halo,
                pltpu.VMEM((tiles // 2, LANES), F32),
                pltpu.VMEM((tiles // 4, LANES), F32),
                pltpu.VMEM((tiles // 4, LANES), F32),
                pltpu.VMEM((tiles, LANES), F32),
                pltpu.VMEM((tiles, LANES), F32),
                pltpu.VMEM((tiles, LANES), F32),
                pltpu.SemaphoreType.DMA((6,)),
                pltpu.SemaphoreType.DMA((4,)),
                pltpu.SemaphoreType.DMA((4,)),
                pltpu.SemaphoreType.DMA,
                pltpu.SemaphoreType.DMA,
                pltpu.SemaphoreType.DMA,
                pltpu.SemaphoreType.DMA,
                pltpu.SemaphoreType.DMA((2,)),
                pltpu.SemaphoreType.REGULAR,
                pltpu.SemaphoreType.REGULAR,
            ],
            compiler_params=pltpu.CompilerParams(collective_id=0, has_side_effects=True, vmem_limit_bytes=56 * 1024 * 1024),
        )(state, zonal, merid, cell, value, weight)

    in_specs = (P("member", "lat", None, None),) + (P("lat", None, None),) * 5
    return jax.shard_map(body, mesh=mesh, in_specs=in_specs, out_specs=P("member", "lat", None, None), check_vma=False)
```

```python
import math

import jax
import jax.numpy as jnp
from jax import lax
from jax.experimental import pallas as pl
from jax.experimental.pallas import tpu as pltpu
from jax.sharding import PartitionSpec as P

MESH = pl.DeviceIdType.MESH
F32 = jnp.float32
BF16 = jnp.bfloat16
HALF_STEP = 0.15
LANES = 128
SIDE_X, SIDE_Y = 8, 4
FAR_X = (4, 5, 3, 6, 2, 7, 1, 0)
FAR_Y = (2, 1, 3, 0)


def split(x):
    high = x.astype(BF16)
    low = (x - high.astype(F32)).astype(BF16)
    return high, low


def dot(a, b):
    return lax.dot_general(a, b, (((1,), (0,)), ((), ())), preferred_element_type=F32)


def dot3(a, b):
    return dot(a[0], b[0]) + (dot(a[0], b[1]) + dot(a[1], b[0]))


def prepare(cells, weights, lons):
    obs = cells.shape[1]
    pick = jnp.where(lax.broadcasted_iota(jnp.int32, (lons, obs), 0) == cells, 1.0, 0.0).astype(BF16)
    diagonal = lax.broadcasted_iota(jnp.int32, (obs, obs), 0) == lax.broadcasted_iota(jnp.int32, (obs, obs), 1)
    return pick, jnp.sqrt(weights), jnp.where(diagonal, 1.0, 0.0)


def analyse(ensemble, values, pick, root_weight, eye):
    count, lons = ensemble.shape
    inflate = count - 1.0
    mean = jnp.sum(ensemble, axis=0, keepdims=True) * (1.0 / count)
    pert = ensemble - mean
    pert_s = split(pert)
    picked = dot(pert_s[0], pick) + dot(pert_s[1], pick)
    mean_s = split(jnp.broadcast_to(mean, (8, lons)))
    obs_mean = dot(mean_s[0], pick) + dot(mean_s[1], pick)
    scaled = picked * root_weight
    target = (values - obs_mean) * root_weight
    scaled_s = split(scaled)
    turned_s = (scaled_s[0].T, scaled_s[1].T)
    gram = dot3(turned_s, scaled_s)
    gram_s = split(gram)
    twice = dot3(gram_s, gram_s)
    cross = dot3(turned_s, pert_s)
    trace = jnp.sum(jnp.sum(scaled * scaled, axis=0, keepdims=True), axis=1, keepdims=True)
    square = jnp.sum(jnp.sum(gram * gram, axis=0, keepdims=True), axis=1, keepdims=True)
    frob = jnp.sqrt(square + 2.0 * inflate * trace + inflate * inflate * count)
    unit = 1.0 / frob
    a0 = inflate * unit
    p1 = 1.5 - 0.5 * a0
    q2 = a0 * p1 * p1
    p2 = 1.5 - 0.5 * q2
    q3 = q2 * p2 * p2
    p3 = 1.5 - 0.5 * q3
    z0 = p1 * p2 * p3
    s = gram * unit
    s_s = split(s)
    s2 = (twice * unit) * unit
    t2 = (p1 * p1 - a0 * p1) * eye + (0.25 * a0 - p1) * s + 0.25 * s2
    m2 = dot3(s_s, split(t2))
    f2 = p2 * eye - 0.5 * m2
    e = p1 * t2 - 0.5 * m2
    f2_s = split(f2)
    u = dot3(f2_s, f2_s) - (0.5 * q2) * (f2 + p2 * eye)
    k = dot3(f2_s, split(e))
    r = -0.5 * (dot3(split(u), split(k)) + p3 * e + (p3 * p2) * eye)
    r_s = split(r)
    core_s = split(dot3(r_s, split(cross)))
    target_s = split(target)
    lead = 2.0 * z0 * dot3(target_s, s_s) + dot3(split(dot3(target_s, split(s2))), r_s)
    shift = unit * (z0 * z0 * dot3(target_s, split(cross)) + dot3(split(lead), core_s))
    gain = jnp.sqrt(inflate * unit)
    return (mean + shift[:1]) + (gain * z0) * pert + (gain * unit) * dot3(scaled_s, core_s)


def around(x, shift):
    lons = x.shape[-1]
    return pltpu.roll(x.reshape(-1, lons), shift, 1).reshape(x.shape)


def slope(x):
    return around(x, x.shape[-1] - 1) - around(x, 1)


def flow(x, zonal):
    return x - (HALF_STEP * (zonal + x)) * slope(x)


def kernel(groups, bands, state, zonal, merid, cell, value, weight, out,
           q, u, v, cells, values, weights, low_in, high_in, low_out, high_out,
           inner, outer, edge, gathered, result, returned,
           load_sem, halo_send, halo_recv, go_send, go_recv, back_send, back_recv, own_sem, ready, band_ready):
    me = lax.axis_index("member")
    band = lax.axis_index("lat")
    members, rows, levels, lons = state.shape
    halves = lons // LANES
    index, odd = me // 2, me % 2
    my_x, my_y = index // SIDE_Y, index % SIDE_Y
    slot = lax.rem(my_y + 2 * (my_x % 2), SIDE_Y)
    my_row = jnp.where(odd == 0, 2 + my_y, jnp.where(slot < 2, 1 + 5 * slot, 7 * (slot - 2)))
    home = my_x * 8 + jnp.where(odd == 0, 2 * my_y, 2 * slot + 1)
    my_level = my_x
    below, above = band > 0, band < bands - 1

    loads = [
        pltpu.make_async_copy(state, q, load_sem.at[0]),
        pltpu.make_async_copy(zonal, u, load_sem.at[1]),
        pltpu.make_async_copy(merid, v, load_sem.at[2]),
        pltpu.make_async_copy(cell.at[my_row], cells, load_sem.at[3]),
        pltpu.make_async_copy(value.at[my_row], values, load_sem.at[4]),
        pltpu.make_async_copy(weight.at[my_row], weights, load_sem.at[5]),
    ]
    for load in loads:
        load.start()

    late = (me == 0) & (band == 0)
    barrier = pltpu.get_barrier_semaphore()

    @pl.when(below)
    def _():
        pl.semaphore_signal(barrier, inc=1, device_id={"lat": band - 1}, device_id_type=MESH)

    @pl.when(above & jnp.logical_not(late))
    def _():
        pl.semaphore_signal(barrier, inc=1, device_id={"lat": band + 1}, device_id_type=MESH)

    @pl.when(jnp.logical_not(late))
    def _():
        def greet(step, carry):
            peer = me + 1 + step
            pl.semaphore_signal(barrier, inc=1, device_id={"member": lax.rem(peer, groups)}, device_id_type=MESH)
            return carry

        lax.fori_loop(0, groups - 1, greet, 0)

    for load in loads[:3]:
        load.wait()

    wind_u, wind_v = u[...], HALF_STEP * v[...]
    old = q[...]
    first, last = old[:, 0], old[:, 7]

    low_out[:members] = first
    low_out[members : 2 * members] = flow(first, wind_u[0]) - wind_v[0] * old[:, 1]
    low_out[2 * members] = wind_v[0]
    high_out[:members] = last
    high_out[members : 2 * members] = flow(last, wind_u[7]) + wind_v[7] * old[:, 6]
    high_out[2 * members] = wind_v[7]

    raw, rest = pl.ds(0, members), pl.ds(members, members + 1)

    def to_low(number, part):
        return pltpu.make_async_remote_copy(
            src_ref=low_out.at[part], dst_ref=high_in.at[part], send_sem=halo_send.at[number], recv_sem=halo_recv.at[number],
            device_id={"lat": band - 1}, device_id_type=MESH)

    def to_high(number, part):
        return pltpu.make_async_remote_copy(
            src_ref=high_out.at[part], dst_ref=low_in.at[part], send_sem=halo_send.at[number], recv_sem=halo_recv.at[number],
            device_id={"lat": band + 1}, device_id_type=MESH)

    def put(block, x, place, every):
        for half in range(halves):
            for member in range(members):
                block[pl.ds(place * 8 + half * members + member, levels, stride=8 * every), :] = (
                    x[member, :, half * LANES : (half + 1) * LANES])

    mid = flow(old[:, 1:7], wind_u[1:7]) - wind_v[1:7] * (old[:, 2:] - old[:, :6])
    new = flow(mid[:, 1:5], wind_u[2:6]) - wind_v[2:6] * (mid[:, 2:] - mid[:, :4])
    for row in range(4):
        put(inner, new[:, row], row, 4)

    after_late = ((me > 0) & (band == 0)) | ((me == 0) & (band == 1))
    pl.semaphore_wait(
        barrier,
        groups - 1 + below.astype(jnp.int32) + above.astype(jnp.int32) - after_late.astype(jnp.int32))

    @pl.when(late)
    def _():
        pl.semaphore_signal(band_ready, inc=1, device_id={"lat": band + 1}, device_id_type=MESH)

        def answer(step, carry):
            pl.semaphore_signal(ready, inc=1, device_id={"member": step}, device_id_type=MESH)
            return carry

        lax.fori_loop(1, groups, answer, 0)

    for number, part in ((0, raw), (2, rest)):

        @pl.when(above)
        def _():
            to_high(number, part).start()

        @pl.when(below & jnp.logical_not(after_late))
        def _():
            to_low(number + 1, part).start()

    far_x = [(lax.rem(my_x + dx, SIDE_X)) for dx in FAR_X]
    turned_y = [[2 * lax.rem(slot + 2 * (x % 2), SIDE_Y) for slot in range(4)] for x in far_x]
    far_y = [(lax.rem(my_y + dy, SIDE_Y)) for dy in FAR_Y]
    mine = pl.ds(pl.multiple_of(me * 8, 8), 8)

    def go(block, tile, peer):
        return pltpu.make_async_remote_copy(
            src_ref=block.at[pl.ds(pl.multiple_of(tile * 8, 8), 8)], dst_ref=gathered.at[mine],
            send_sem=go_send, recv_sem=go_recv, device_id={"member": peer}, device_id_type=MESH)

    for x in far_x:
        for y in far_y:
            tile = x * SIDE_Y + y

            @pl.when(((tile > 0) | (band > 0)) & (2 * tile != me))
            def _():
                go(inner, tile, 2 * tile).start()

    @pl.when(below & after_late)
    def _():
        pl.semaphore_wait(band_ready, 1)
        to_low(1, raw).start()
        to_low(3, rest).start()

    def send_outer(block, first_slot):
        for x, turned in zip(far_x, turned_y):
            for row in range(2):
                peer = x * 8 + (turned[first_slot + row] + 1)

                @pl.when(peer != me)
                def _():
                    go(block, x * 2 + row, peer).start()

    @pl.when(below)
    def _():
        to_high(0, raw).wait_recv()

    @pl.when(band == 0)
    def _():
        low_in[...] = jnp.zeros_like(low_in)

    @pl.when(above)
    def _():
        to_low(1, raw).wait_recv()

    @pl.when(band == bands - 1)
    def _():
        high_in[...] = jnp.zeros_like(high_in)

    row0 = flow(first, wind_u[0]) - wind_v[0] * (old[:, 1] - low_in[:members])
    row7 = flow(last, wind_u[7]) - wind_v[7] * (high_in[:members] - old[:, 6])
    put(outer, flow(mid[:, 0], wind_u[1]) - wind_v[1] * (mid[:, 1] - row0), 0, 2)
    put(outer, flow(mid[:, 5], wind_u[6]) - wind_v[6] * (row7 - mid[:, 4]), 1, 2)
    send_outer(outer, 0)

    @pl.when(below)
    def _():
        to_high(2, rest).wait_recv()

    @pl.when(above)
    def _():
        to_low(3, rest).wait_recv()

    before = low_in[members : 2 * members] - low_in[2 * members] * first
    after = high_in[members : 2 * members] + high_in[2 * members] * last
    put(edge, flow(row0, wind_u[0]) - wind_v[0] * (mid[:, 0] - before), 0, 2)
    put(edge, flow(row7, wind_u[7]) - wind_v[7] * (after - mid[:, 5]), 1, 2)
    send_outer(edge, 2)

    def keep(block, tile):
        return pltpu.make_async_copy(block.at[pl.ds(pl.multiple_of(tile * 8, 8), 8)], gathered.at[mine], own_sem.at[0])

    @pl.when(odd == 0)
    def _():
        keep(inner, index).start()

    @pl.when((odd == 1) & (slot < 2))
    def _():
        keep(outer, my_x * 2 + slot).start()

    @pl.when((odd == 1) & (slot >= 2))
    def _():
        keep(edge, my_x * 2 + slot - 2).start()

    for load in loads[3:]:
        load.wait()
    region = pl.ds(my_level, 1)
    observed = values[region, :]
    prepared = prepare(cells[region, :], weights[region, :], lons)

    @pl.when((me > 0) & (band == 0))
    def _():
        pl.semaphore_wait(ready, 1)
        go(inner, 0, 0).start()

    keep(inner, index).wait()
    others = pl.ds(0, (groups - 1) * 8)
    pltpu.make_async_copy(gathered.at[others], gathered.at[others], go_recv).wait()

    ensemble = jnp.concatenate(
        [jnp.concatenate(
            [gathered[pl.ds(half * members + member, groups, stride=8), :] for member in range(members)], axis=0)
         for half in range(halves)], axis=1)
    analysed = analyse(ensemble, observed, *prepared)
    for half in range(halves):
        for member in range(members):
            result[pl.ds(half * members + member, groups, stride=8), :] = (
                analysed[member * groups : (member + 1) * groups, half * LANES : (half + 1) * LANES])

    there = pl.ds(pl.multiple_of(home * 8, 8), 8)

    def give(peer):
        return pltpu.make_async_remote_copy(
            src_ref=result.at[pl.ds(pl.multiple_of(peer * 8, 8), 8)], dst_ref=returned.at[there],
            send_sem=back_send, recv_sem=back_recv, device_id={"member": peer}, device_id_type=MESH)

    for x in far_x:
        for y in far_y:
            for core in range(2):
                peer = x * 8 + 2 * y + core
                if (x is far_x[-1]) and (y is far_y[-1]):

                    @pl.when(odd != core)
                    def _():
                        give(peer).start()
                else:
                    give(peer).start()

    own = pltpu.make_async_copy(result.at[mine], returned.at[there], own_sem.at[1])
    own.start()
    own.wait()
    pltpu.make_async_copy(returned.at[others], returned.at[others], back_recv).wait()

    for row, place, core in ((2, 0, 0), (3, 1, 0), (4, 2, 0), (5, 3, 0), (1, 0, 1), (6, 1, 1), (0, 2, 1), (7, 3, 1)):
        for half in range(halves):
            for member in range(members):
                start = (2 * place + core) * 8 + half * members + member
                out[member, row, :, half * LANES : (half + 1) * LANES] = returned[pl.ds(start, levels, stride=64), :]

    @pl.when(below)
    def _():
        to_low(1, raw).wait_send()
        to_low(3, rest).wait_send()

    @pl.when(above)
    def _():
        to_high(0, raw).wait_send()
        to_high(2, rest).wait_send()

    pltpu.make_async_copy(gathered.at[others], gathered.at[others], go_send).wait()
    pltpu.make_async_copy(returned.at[others], returned.at[others], back_send).wait()


def solution(mesh):
    groups, bands = mesh.shape["member"], mesh.shape["lat"]
    assert groups == 2 * SIDE_X * SIDE_Y

    def body(state, zonal, merid, cell, value, weight):
        members, rows, levels, lons = state.shape
        obs = cell.shape[-1]
        halo = pltpu.VMEM((2 * members + 1, levels, lons), F32)
        tiles = groups * 8
        return pl.pallas_call(
            lambda *refs: kernel(groups, bands, *refs),
            out_shape=pltpu.VMEM(state.shape, F32),
            in_specs=[pl.BlockSpec(memory_space=pltpu.HBM)] * 6,
            out_specs=pl.BlockSpec(memory_space=pltpu.VMEM),
            scratch_shapes=[
                pltpu.VMEM(state.shape, F32),
                pltpu.VMEM(zonal.shape, F32),
                pltpu.VMEM(merid.shape, F32),
                pltpu.VMEM((levels, obs), jnp.int32),
                pltpu.VMEM((levels, obs), F32),
                pltpu.VMEM((levels, obs), F32),
                halo, halo, halo, halo,
                pltpu.VMEM((tiles // 2, LANES), F32),
                pltpu.VMEM((tiles // 4, LANES), F32),
                pltpu.VMEM((tiles // 4, LANES), F32),
                pltpu.VMEM((tiles, LANES), F32),
                pltpu.VMEM((tiles, LANES), F32),
                pltpu.VMEM((tiles, LANES), F32),
                pltpu.SemaphoreType.DMA((6,)),
                pltpu.SemaphoreType.DMA((4,)),
                pltpu.SemaphoreType.DMA((4,)),
                pltpu.SemaphoreType.DMA,
                pltpu.SemaphoreType.DMA,
                pltpu.SemaphoreType.DMA,
                pltpu.SemaphoreType.DMA,
                pltpu.SemaphoreType.DMA((2,)),
                pltpu.SemaphoreType.REGULAR,
                pltpu.SemaphoreType.REGULAR,
            ],
            compiler_params=pltpu.CompilerParams(collective_id=0, has_side_effects=True, vmem_limit_bytes=56 * 1024 * 1024),
        )(state, zonal, merid, cell, value, weight)

    in_specs = (P("member", "lat", None, None),) + (P("lat", None, None),) * 5
    return jax.shard_map(body, mesh=mesh, in_specs=in_specs, out_specs=P("member", "lat", None, None), check_vma=False)
```
